512 devices in a mesh: src: 32 (over x, z), tgt: 16 (over y, core).
Axes of the slice: x: 4, y: 8, z: 8, core: 2. Of those that a mesh axis runs over, the one named last changes fastest.
Arguments:
- sources: bfloat16 [262144, 64], P(('src', 'tgt')), may hold values from -2.09375 to 2.09375
- targets: bfloat16 [262144, 64], P('tgt'), may hold values from -2.09375 to 2.09375
- potential: float32 [262144], P('src'), may hold values from -1 to 112
- block_map: int32 [1024, 20], P('src'), may hold values from -1 to 1023, as said below
- counts: int32 [1024], P('src'), may hold values from 10 to 20, as said below
- step_history: float32 [8, 262144], P(None, ('src', 'tgt')), may hold values from -13 to 13
- slope_history: float32 [8, 262144], P(None, ('src', 'tgt')), may hold values from -64 to 64, as said below
Outputs:
- gradient: float32 [262144], P(('src', 'tgt'))
- direction: float32 [262144], P(('src', 'tgt'))
- target_potential: float32 [262144], P('tgt')
The draws below stay inside these ranges and needn't reach their ends.
Inputs may be any that keep to these rules, and one draw needn't show every extreme that they name: `block_map`: row b lists counts[b] different target block numbers in slots 0 to counts[b] - 1 and -1 in the other slots; every target block is listed in some row. `counts`: some source block lists exactly 20 target blocks in every draw. For every k the sum over all points of step_history[k] slope_history[k] is positive.
All inputs are finite; a program needn't handle non-finite values.
Results may differ from the reference program's by a relative error of at most 0.0008.
Values may be sent and summed in bfloat16 or wider, within the bound.
No kernel may reach another device: no remote copies, remote signals or barrier semaphores. Data moves between devices by JAX's collectives and lax.ppermute only.
A program may use at most 64 MiB of HBM per device.

```python
import jax
import jax.numpy as jnp
from jax import lax

D = 64
BLOCK = 256
KMAX = 20
HIST = 8
NSB = 1024
NTB = 1024
NS = 262144
NT = 262144


def block_layout(key):
    seeded = jax.random.fold_in(key, 101)
    key_count, key_first, key_second, key_mixing, key_shuffle = jax.random.split(seeded, 5)
    lowest = max(KMAX // 2, 1)
    block_index = jnp.arange(NSB, dtype=jnp.int32)
    number = jax.random.randint(key_count, (NSB,), lowest, KMAX + 1)
    number = jnp.where(block_index == 0, KMAX, number)
    first_draw = jax.random.randint(key_first, (NSB,), 0, NTB)
    second_draw = jax.random.randint(key_second, (NSB,), 0, NTB)
    mixing = jax.random.randint(key_mixing, (NSB,), 0, 2)
    center = jnp.where(mixing == 1, first_draw * second_draw // NTB, first_draw)
    window = 2 * KMAX
    spacing = max(NTB // window, 1)
    offsets = jnp.arange(window, dtype=jnp.int32) - KMAX
    candidate = (center[:, None] + offsets[None, :] * spacing) % NTB
    homeward = block_index % NTB
    ranking = jax.random.randint(key_shuffle, (NSB, window), 0, 2 ** 20) * window + offsets[None, :] + KMAX
    ranking = jnp.where(candidate == homeward[:, None], 2 ** 30, ranking)
    ordering = jnp.argsort(ranking, axis=1)
    others = jnp.take_along_axis(candidate, ordering, axis=1)[:, :KMAX - 1]
    listing = jnp.concatenate([homeward[:, None], others], axis=1)
    slot_index = jnp.arange(KMAX, dtype=jnp.int32)
    listing = jnp.where(slot_index[None, :] < number[:, None], listing, -1)
    return (listing.astype(jnp.int32), number.astype(jnp.int32))


def draw_block_map(key, part):
    return block_layout(key)[0]


def draw_counts(key, part):
    return block_layout(key)[1]


def draw_potential(key, part):
    seeded = jax.random.fold_in(key, 303)
    key_noise = jax.random.fold_in(seeded, 0)
    point_index = jnp.arange(NS, dtype=jnp.int32)
    ramp_term = jnp.log(1.0 + 2.0 * point_index.astype(jnp.float32) / (NS - 1))
    noise = 0.5 * jnp.clip(jax.random.normal(key_noise, (NS,), jnp.float32), -3.0, 3.0)
    values = 0.5 * (noise + ramp_term)
    return values.astype(jnp.float32)


def history_pair(key):
    seeded = jax.random.fold_in(key, 202)
    key_steps, key_factor = jax.random.split(seeded, 2)
    point_index = jnp.arange(NS, dtype=jnp.int32).astype(jnp.float32)
    ramp_term = 1.0 + 2.0 * point_index / (NS - 1)
    steps_drawn = 0.5 * ramp_term[None, :] * jnp.clip(jax.random.normal(key_steps, (HIST, NS), jnp.float32), -4.0, 4.0)
    factor = jnp.exp(jax.random.uniform(key_factor, (HIST, NS), jnp.float32, jnp.log(0.3), jnp.log(3.0)))
    return (steps_drawn, steps_drawn * factor)


def draw_step_history(key, part):
    return history_pair(key)[0].astype(jnp.float32)


def draw_slope_history(key, part):
    return history_pair(key)[1].astype(jnp.float32)


def steps_of(rng, extent, cuts, least, top_value):
    level, own = 1.0, jax.random.fold_in(rng, 6)
    for position, shards_of in cuts:
        draws = jnp.exp(jax.random.uniform(jax.random.fold_in(own, position), (shards_of,), jnp.float32, least / len(cuts), top_value / len(cuts)))
        level = level * jnp.repeat(draws, extent[position] // shards_of).reshape([-1 if axis == position else 1 for axis in range(len(extent))])
    return level


def gaussian(stream_key, extent, deviation, bound, pieces=(), held_as=jnp.bfloat16):
    loudness = steps_of(stream_key, extent, pieces, -0.22, 0.18) if pieces else 1.0
    values = jax.random.normal(stream_key, extent, jnp.float32) * deviation * loudness
    return jnp.minimum(jnp.maximum(values, -bound), bound).astype(held_as)


def setup_inputs(seed: int = 0) -> dict:
    key_of = jax.random.split(jax.random.key(seed), 8)
    return {
        "sources": gaussian(key_of[0], (NS, D), 0.35, 2.09375, ((0, 512),)),
        "targets": gaussian(key_of[1], (NT, D), 0.35, 2.09375, ((0, 16),)),
        "potential": draw_potential(jax.random.fold_in(key_of[7], 71), 0),
        "block_map": draw_block_map(jax.random.fold_in(key_of[7], 71), 0),
        "counts": draw_counts(jax.random.fold_in(key_of[7], 71), 0),
        "step_history": draw_step_history(jax.random.fold_in(key_of[7], 71), 0),
        "slope_history": draw_slope_history(jax.random.fold_in(key_of[7], 71), 0),
    }


entropy = 0.5


def block_scores(source_tiles, potential_tiles, target_tiles, block_map, counts, block):
    slot_index = jnp.arange(KMAX, dtype=jnp.int32)
    live = slot_index < counts[block]
    safe = jnp.where(live, block_map[block], 0).astype(jnp.int32)
    tiles = target_tiles[safe].astype(jnp.float32)
    rows_in = source_tiles[block].astype(jnp.float32)
    product = jnp.einsum("id,kjd->kij", rows_in, tiles)
    return (potential_tiles[block][None, :, None] + product) / entropy, live, safe


def reference(sources, targets, potential, block_map, counts, step_history, slope_history):
    source_tiles = sources.reshape(NSB, BLOCK, D)
    target_tiles = targets.reshape(NTB, BLOCK, D)
    potential_tiles = potential.reshape(NSB, BLOCK)
    blocks_all = jnp.arange(NSB, dtype=jnp.int32)

    def column_step(carry, block):
        peak, total = carry
        scores, live, safe = block_scores(source_tiles, potential_tiles, target_tiles, block_map, counts, block)
        tile_peak = jnp.max(scores, axis=1)
        tile_total = jnp.sum(jnp.exp(scores - tile_peak[:, None, :]), axis=1)
        target_ids = jnp.where(live, safe, NTB).astype(jnp.int32)
        old_peak = peak[target_ids]
        new_peak = jnp.maximum(old_peak, tile_peak)
        new_total = total[target_ids] * jnp.exp(old_peak - new_peak) + tile_total * jnp.exp(tile_peak - new_peak)
        return (peak.at[target_ids].set(new_peak), total.at[target_ids].set(new_total)), None

    start_peak = jnp.full((NTB + 1, BLOCK), -1e30, jnp.float32)
    start_total = jnp.zeros((NTB + 1, BLOCK), jnp.float32)
    (peak, total), _ = lax.scan(column_step, (start_peak, start_total), blocks_all)
    log_tiles = peak[:NTB] + jnp.log(total[:NTB])
    target_potential = -entropy * log_tiles.reshape(NT)

    def row_step(carry, block):
        scores, live, safe = block_scores(source_tiles, potential_tiles, target_tiles, block_map, counts, block)
        weights = jnp.exp(scores - log_tiles[safe][:, None, :])
        weights = jnp.where(live[:, None, None], weights, 0.0)
        return carry, jnp.sum(weights, axis=(0, 2))

    _, masses = lax.scan(row_step, 0.0, blocks_all)
    gradient = 1.0 - (NS / NT) * masses.reshape(NS)

    inverse = []
    for index in range(HIST):
        inverse.append(1.0 / jnp.sum(step_history[index] * slope_history[index]))
    scale = jnp.sum(step_history[HIST - 1] * slope_history[HIST - 1]) / jnp.sum(slope_history[HIST - 1] * slope_history[HIST - 1])
    search = gradient
    alphas = [None] * HIST
    for index in reversed(range(HIST)):
        alphas[index] = inverse[index] * jnp.sum(step_history[index] * search)
        search = search - alphas[index] * slope_history[index]
    result = scale * search
    for index in range(HIST):
        beta_value = inverse[index] * jnp.sum(slope_history[index] * result)
        result = result + (alphas[index] - beta_value) * step_history[index]
    direction = -result
    return gradient, direction, target_potential
```

```python
import functools

import jax
import jax.numpy as jnp
from jax import lax
from jax.experimental import pallas as pl
from jax.experimental.pallas import tpu as pltpu
from jax.sharding import Mesh
from jax.sharding import PartitionSpec as P

BLOCK = 256
HALF = 128
TGT = ("tgt_0", "tgt_1")
SRC = ("src_0", "src_1")
SRC_TGT = ("src_0", "src_1", "tgt_0", "tgt_1")
NEG = -1e30
LOG2E = 1.4426950408889634
LN2 = 0.6931471805599453
entropy = 0.5
SCALE = LOG2E / entropy
UNROLL = 2
F32 = jnp.float32

VMEM = pl.BlockSpec(memory_space=pltpu.VMEM)
SMEM = pl.BlockSpec(memory_space=pltpu.SMEM)


def call(body, out_shape, ins, outs, scratch=(), cost=None):
    return pl.pallas_call(
        body,
        out_shape=out_shape,
        in_specs=ins,
        out_specs=outs,
        scratch_shapes=list(scratch),
        cost_estimate=cost,
        compiler_params=pltpu.CompilerParams(vmem_limit_bytes=40 * 2**20),
    )


def sds(shape, dtype=F32):
    return jax.ShapeDtypeStruct(shape, dtype)


def nt(a, b, precision=None):
    return lax.dot_general(
        a, b, (((1,), (1,)), ((), ())), precision=precision, preferred_element_type=F32
    )


def swap(x, axis):
    return lax.all_to_all(x, axis, 0, 0, tiled=True)


def share(x, axis):
    return swap(jnp.broadcast_to(x[None], (lax.axis_size(axis), *x.shape)), axis)


def listing_kernel(blocks, own_blocks, rank, block_map, counts, src, tgt, total):
    first = rank[0] * own_blocks

    def of_block(b, n):
        def of_slot(k, n):
            local = block_map[b, k] - first
            src[n] = b
            tgt[n] = local
            mine = (local >= 0) & (local < own_blocks)
            return n + mine.astype(jnp.int32)

        return lax.fori_loop(0, counts[b], of_slot, n)

    n = lax.fori_loop(0, blocks, of_block, jnp.int32(0))
    total[0] = n
    for extra in range(UNROLL):
        src[n + extra] = blocks
        tgt[n + extra] = own_blocks


def masked_rows(x, mask, b):
    piece = x[lax.shift_right_logical(b, 1)].reshape(BLOCK // 16, 16, HALF)
    lanes = mask[pl.ds(pl.multiple_of(lax.rem(b, 2) * 16, 16), 16), :]
    return (piece * lanes[None]).reshape(BLOCK, HALF)


def column_kernel(blocks, own_blocks, src, tgt, total, x, t, pot, gram, mask, out, peak, acc):
    peak[...] = jnp.full(peak.shape, NEG, F32)
    acc[...] = jnp.zeros(acc.shape, F32)
    pairs = total[0]

    def turn(step, carry):
        found = []
        for u in range(UNROLL):
            b_all = src[step * UNROLL + u]
            t_all = tgt[step * UNROLL + u]
            b = jnp.minimum(b_all, blocks - 1)
            tb = jnp.minimum(t_all, own_blocks - 1)
            rows = masked_rows(x, mask, b)
            pieces = []
            for h in range(2):
                line = pot[pl.ds(2 * b + h, 1), :] * SCALE
                pieces.append(jnp.transpose(jnp.broadcast_to(line, (HALF, HALF))))
            shift = jnp.concatenate(pieces, axis=0)
            for h in range(2):
                cols = t[pl.ds(pl.multiple_of(tb * BLOCK + h * HALF, HALF), HALF), :]
                s = nt(rows, cols) * SCALE + shift
                s = s.reshape(BLOCK // 8, 8, HALF)
                top = jnp.max(s, axis=0)
                part = jnp.sum(jnp.exp2(s - top[None]), axis=0)
                found.append((t_all, h, top, part))
        for t_all, h, top, part in found:
            at = (pl.ds(pl.multiple_of(t_all * 8, 8), 8), slice(h * HALF, (h + 1) * HALF))
            old = peak[at]
            new = jnp.maximum(old, top)
            acc[at] = acc[at] * jnp.exp2(old - new) + part * jnp.exp2(top - new)
            peak[at] = new
        return carry

    lax.fori_loop(0, (pairs + UNROLL - 1) // UNROLL, turn, 0)

    row = lax.broadcasted_iota(jnp.int32, (8, HALF), 0)
    moments = jnp.broadcast_to(gram[...], (8, HALF))

    def finish(p, carry):
        tile = jnp.where(row == 4, moments, 0.0)
        for r in range(4):
            at = (
                pl.ds(pl.multiple_of((2 * p + r // 2) * 8, 8), 8),
                slice((r % 2) * HALF, (r % 2 + 1) * HALF),
            )
            tops = peak[at]
            top = jnp.max(tops, axis=0, keepdims=True)
            whole = jnp.sum(acc[at] * jnp.exp2(tops - top), axis=0, keepdims=True)
            level = jnp.where(whole > 0.0, top + jnp.log2(jnp.maximum(whole, 1e-38)), NEG)
            tile = jnp.where(row == r, level, tile)
        out[p] = tile
        return carry

    lax.fori_loop(0, own_blocks // 2, finish, 0, unroll=4)


def combine_kernel(peers, arrived, out, gram):
    top = arrived[0]
    for p in range(1, peers):
        top = jnp.maximum(top, arrived[p])
    whole = jnp.zeros_like(top)
    plain = jnp.zeros_like(top)
    for p in range(peers):
        whole = whole + jnp.exp2(arrived[p] - top)
        plain = plain + arrived[p]
    level = (top + jnp.log2(whole))[:4]
    for p in range(peers):
        out[p] = level
    gram[...] = plain[4:5]


def row_kernel(blocks, own_blocks, src, tgt, total, x, t, pot, level, mask, out, acc):
    acc[...] = jnp.zeros(acc.shape, F32)
    pairs = total[0]

    def turn(step, carry):
        found = []
        for u in range(UNROLL):
            b_all = src[step * UNROLL + u]
            t_all = tgt[step * UNROLL + u]
            b = jnp.minimum(b_all, blocks - 1)
            tb = jnp.minimum(t_all, own_blocks - 1)
            rows = masked_rows(x, mask, b)
            lines = [pot[pl.ds(2 * b + h, 1), :] * SCALE for h in range(2)]
            line = jnp.concatenate(lines, axis=1)
            parts = None
            for h in range(2):
                cols = t[pl.ds(pl.multiple_of(tb * BLOCK + h * HALF, HALF), HALF), :]
                log_line = level[
                    lax.shift_right_logical(tb, 1), pl.ds(lax.rem(tb, 2) * 2 + h, 1), :
                ]
                shift = jnp.transpose(jnp.broadcast_to(log_line, (HALF, HALF)))
                s = nt(cols, rows) * SCALE + line
                e = jnp.exp2(s - jnp.concatenate([shift, shift], axis=1))
                part = jnp.sum(e.reshape(HALF // 8, 8, BLOCK), axis=0)
                parts = part if parts is None else parts + part
            found.append((b_all, parts))
        for b_all, parts in found:
            at = pl.ds(pl.multiple_of(b_all * 8, 8), 8)
            acc[at, :] = acc[at, :] + parts
        return carry

    lax.fori_loop(0, (pairs + UNROLL - 1) // UNROLL, turn, 0)

    def finish(p, carry):
        for half in range(2):
            at = pl.ds(pl.multiple_of((2 * p + half) * 8, 8), 8)
            sums = jnp.sum(acc[at, :], axis=0, keepdims=True)
            for h in range(2):
                out[p, 2 * half + h : 2 * half + h + 1, :] = sums[:, h * HALF : (h + 1) * HALF]
        return carry

    lax.fori_loop(0, blocks // 2, finish, 0, unroll=4)


def gradient_kernel(peers, ratio, arrived, steps, slopes, gradient, dots):
    mass = arrived[0]
    for p in range(1, peers):
        mass = mass + arrived[p]
    grad = 1.0 - ratio * mass
    gradient[...] = grad
    line = jnp.concatenate([grad[r : r + 1] for r in range(4)], axis=1)
    lane = lax.broadcasted_iota(jnp.int32, (8, HALF), 1)
    row = lax.broadcasted_iota(jnp.int32, (8, HALF), 0)
    step_dots = jnp.sum(steps[...] * line, axis=1, keepdims=True)
    slope_dots = jnp.sum(slopes[...] * line, axis=1, keepdims=True)
    spread = jnp.where(lane == row, step_dots, 0.0) + jnp.where(lane == row + 8, slope_dots, 0.0)
    value = jnp.sum(spread, axis=0, keepdims=True)
    for p in range(peers):
        dots[p] = value


def pass_on_kernel(peers, given, arrived, out):
    value = arrived[0]
    for p in range(1, peers):
        value = value + arrived[p]
    for p in range(given):
        out[p] = value


def recursion_kernel(stored, gram, out):
    lane = lax.broadcasted_iota(jnp.int32, (1, HALF), 1)

    def unit(k):
        return jnp.where(lane == k, 1.0, 0.0).astype(F32)

    def cross(k, m):
        return gram[0, 8 * k + m]

    def slope(k, m):
        return gram[0, 64 + 8 * k + m]

    def full(value):
        return jnp.full((1, HALF), value, F32)

    rho = [1.0 / full(cross(k, k)) for k in range(stored)]
    gamma = full(cross(stored - 1, stored - 1)) / full(slope(stored - 1, stored - 1))
    alpha = [None] * stored
    for k in reversed(range(stored)):
        value = unit(k)
        for m in range(k + 1, stored):
            value = value - cross(k, m) * alpha[m]
        alpha[k] = value * rho[k]
    delta = [None] * stored
    for k in range(stored):
        value = unit(8 + k)
        for m in range(stored):
            value = value - slope(k, m) * alpha[m]
        value = value * gamma
        for m in range(k):
            value = value + cross(m, k) * delta[m]
        delta[k] = alpha[k] - value * rho[k]
    for k in range(stored):
        out[k : k + 1, :] = -delta[k]
        out[8 + k : 9 + k, :] = gamma * alpha[k]
    out[16:17, :] = -gamma


def direction_kernel(peers, arrived, forms, gradient, steps, slopes, out):
    dots = arrived[0]
    for p in range(1, peers):
        dots = dots + arrived[p]
    weights = jnp.sum(forms[:16, :] * dots, axis=1, keepdims=True)
    mix = weights[:8] * steps[...] + weights[8:16] * slopes[...]
    mix = jnp.sum(mix, axis=0, keepdims=True)
    line = jnp.concatenate([mix[:, r * HALF : (r + 1) * HALF] for r in range(4)], axis=0)
    out[...] = forms[16:17, :] * gradient[...] + line


def per_device(sources, targets, potential, block_map, counts, step_history, slope_history):
    src_size, tgt_size = lax.axis_size(SRC), lax.axis_size(TGT)
    blocks = potential.shape[0] // BLOCK
    own_blocks = targets.shape[0] // BLOCK
    listed = block_map.shape[1]
    stored = step_history.shape[0]
    pieces = sources.shape[0] // BLOCK
    assert pieces == 2

    packed = jnp.concatenate([sources[:BLOCK], sources[BLOCK:]], axis=1)
    x = share(packed, TGT)
    t = jnp.concatenate([targets, targets], axis=1)
    pot = potential.reshape(-1, HALF)
    lane = jnp.arange(HALF, dtype=jnp.int32)[None, :] // 64
    mask_row = jnp.arange(32, dtype=jnp.int32)[:, None] // 16
    mask = (lane == mask_row).astype(jnp.bfloat16)

    highest = lax.Precision.HIGHEST
    cross = nt(step_history, slope_history, highest)
    slopes = nt(slope_history, slope_history, highest)
    moments = jnp.concatenate([cross.reshape(1, -1), slopes.reshape(1, -1)], axis=1)
    gram_part = jnp.sum(share(moments, TGT), axis=0)

    rank = lax.axis_index(TGT).astype(jnp.int32).reshape(1)
    slots = blocks * listed + UNROLL
    src, tgt, total = call(
        functools.partial(listing_kernel, blocks, own_blocks),
        (sds((slots,), jnp.int32), sds((slots,), jnp.int32), sds((1,), jnp.int32)),
        [SMEM] * 3,
        [SMEM] * 3,
    )(rank, block_map, counts)

    levels = call(
        functools.partial(column_kernel, blocks, own_blocks),
        sds((src_size, 8, HALF)),
        [SMEM] * 3 + [VMEM] * 5,
        VMEM,
        [pltpu.VMEM((8 * own_blocks + 8, BLOCK), F32)] * 2,
    )(src, tgt, total, x, t, pot, gram_part, mask)

    level, gram = call(
        functools.partial(combine_kernel, src_size),
        (sds((src_size, 4, HALF)), sds((1, HALF))),
        [VMEM],
        [VMEM] * 2,
    )(swap(levels, SRC))
    level = swap(level, SRC)
    target_potential = (-entropy * LN2) * level.reshape(-1)

    forms = call(
        functools.partial(recursion_kernel, stored), sds((24, HALF)), [SMEM], VMEM
    )(gram)

    masses = call(
        functools.partial(row_kernel, blocks, own_blocks),
        sds((tgt_size, 4, HALF)),
        [SMEM] * 3 + [VMEM] * 5,
        VMEM,
        [pltpu.VMEM((8 * blocks + 8, BLOCK), F32)],
    )(src, tgt, total, x, t, pot, level, mask)

    ratio = blocks * src_size / (own_blocks * tgt_size)
    gradient, dots = call(
        functools.partial(gradient_kernel, tgt_size, ratio),
        (sds((4, HALF)), sds((tgt_size, 1, HALF))),
        [VMEM] * 3,
        [VMEM] * 2,
    )(swap(masses, TGT), step_history, slope_history)
    dots = call(
        functools.partial(pass_on_kernel, tgt_size, src_size),
        sds((src_size, 1, HALF)),
        [VMEM],
        VMEM,
    )(swap(dots, TGT))
    direction = call(
        functools.partial(direction_kernel, src_size), sds((4, HALF)), [VMEM] * 5, VMEM
    )(swap(dots, SRC), forms, gradient, step_history, slope_history)
    return (gradient.reshape(-1), direction.reshape(-1), target_potential)


def solution(mesh):
    split = Mesh(mesh.devices.reshape(4, 8, 8, 2), ("src_0", "src_1", "tgt_0", "tgt_1"))
    in_specs = (
        P(SRC_TGT, None),
        P(TGT, None),
        P(SRC),
        P(SRC, None),
        P(SRC),
        P(None, SRC_TGT),
        P(None, SRC_TGT),
    )
    out_specs = (P(SRC_TGT), P(SRC_TGT), P(TGT))
    return jax.shard_map(
        per_device, mesh=split, in_specs=in_specs, out_specs=out_specs, check_vma=False
    )
```

```python
import functools

import jax
import jax.numpy as jnp
from jax import lax
from jax.experimental import pallas as pl
from jax.experimental.pallas import tpu as pltpu
from jax.sharding import Mesh
from jax.sharding import PartitionSpec as P

BLOCK = 256
HALF = 128
TGT = ("tgt_0", "tgt_1")
SRC = ("src_0", "src_1")
SRC_TGT = ("src_0", "src_1", "tgt_0", "tgt_1")
NEG = -1e30
LOG2E = 1.4426950408889634
LN2 = 0.6931471805599453
entropy = 0.5
SCALE = LOG2E / entropy
UNROLL = 2
F32 = jnp.float32

VMEM = pl.BlockSpec(memory_space=pltpu.VMEM)
SMEM = pl.BlockSpec(memory_space=pltpu.SMEM)


def call(body, out_shape, ins, outs, scratch=(), cost=None):
    return pl.pallas_call(
        body,
        out_shape=out_shape,
        in_specs=ins,
        out_specs=outs,
        scratch_shapes=list(scratch),
        cost_estimate=cost,
        compiler_params=pltpu.CompilerParams(vmem_limit_bytes=24 * 2**20),
    )


def sds(shape, dtype=F32):
    return jax.ShapeDtypeStruct(shape, dtype)


def nn(a, b):
    return jnp.dot(a, b, preferred_element_type=F32)


def nt(a, b, precision=None):
    return lax.dot_general(
        a, b, (((1,), (1,)), ((), ())), precision=precision, preferred_element_type=F32
    )


def swap(x, axis):
    return lax.all_to_all(x, axis, 0, 0, tiled=True)


def share(x, axis):
    return swap(jnp.broadcast_to(x[None], (lax.axis_size(axis), *x.shape)), axis)


def listing_kernel(blocks, own_blocks, rank, block_map, counts, src, tgt, total):
    first = rank[0] * own_blocks

    def of_block(b, n):
        count = counts[b]
        for k in range(block_map.shape[1]):
            local = block_map[b, k] - first
            src[n] = b
            tgt[n] = local
            mine = (k < count) & (local >= 0) & (local < own_blocks)
            n = n + mine.astype(jnp.int32)
        return n

    n = lax.fori_loop(0, blocks, of_block, jnp.int32(0))
    total[0] = n
    for extra in range(UNROLL):
        src[n + extra] = blocks
        tgt[n + extra] = own_blocks


def lay_out(rank, mine, other, mask, rows):
    core = rank[1]
    for arrived, side in ((mine, core), (other, 1 - core)):
        for y in range(arrived.shape[0]):
            piece = arrived[y].reshape(BLOCK // 16, 16, HALF)
            for half in range(2):
                lanes = mask[half * 16 : half * 16 + 16, :]
                rows[4 * y + 2 * side + half] = (piece * lanes[None]).reshape(BLOCK, HALF)


def column_kernel(
    blocks, own_blocks, rank, src, tgt, total, mine, other, t, pot, mask, out, x, peak, acc
):
    lay_out(rank, mine, other, mask, x)
    peak[...] = jnp.full(peak.shape, NEG, F32)
    acc[...] = jnp.zeros(acc.shape, F32)
    live = total[0]

    def turn(step, carry):
        found = []
        for u in range(UNROLL):
            b_all = src[step * UNROLL + u]
            t_all = tgt[step * UNROLL + u]
            b = jnp.minimum(b_all, blocks - 1)
            tb = jnp.minimum(t_all, own_blocks - 1)
            rows = x[b]
            pieces = []
            for h in range(2):
                line = pot[pl.ds(2 * b + h, 1), :] * SCALE
                pieces.append(jnp.transpose(jnp.broadcast_to(line, (HALF, HALF))))
            shift = jnp.concatenate(pieces, axis=0)
            for h in range(2):
                cols = t[:, pl.ds(pl.multiple_of(tb * BLOCK + h * HALF, HALF), HALF)]
                s = nn(rows, cols) * SCALE + shift
                s = s.reshape(BLOCK // 8, 8, HALF)
                top = jnp.max(s, axis=0)
                part = jnp.sum(jnp.exp2(s - top[None]), axis=0)
                found.append((t_all, h, top, part))
        for t_all, h, top, part in found:
            at = (pl.ds(pl.multiple_of(t_all * 8, 8), 8), slice(h * HALF, (h + 1) * HALF))
            old = peak[at]
            new = jnp.maximum(old, top)
            acc[at] = acc[at] * jnp.exp2(old - new) + part * jnp.exp2(top - new)
            peak[at] = new
        return carry

    lax.fori_loop(0, (live + UNROLL - 1) // UNROLL, turn, 0)

    def finish(p, carry):
        for r in range(4):
            at = (
                pl.ds(pl.multiple_of((2 * p + r // 2) * 8, 8), 8),
                slice((r % 2) * HALF, (r % 2 + 1) * HALF),
            )
            tops = peak[at]
            top = jnp.max(tops, axis=0, keepdims=True)
            whole = jnp.sum(acc[at] * jnp.exp2(tops - top), axis=0, keepdims=True)
            level = jnp.where(whole > 0.0, top + jnp.log2(jnp.maximum(whole, 1e-38)), NEG)
            out[p, r : r + 1, :] = level
        return carry

    lax.fori_loop(0, own_blocks // 2, finish, 0, unroll=4)


def combine_kernel(peers, arrived, out):
    top = arrived[0]
    for p in range(1, peers):
        top = jnp.maximum(top, arrived[p])
    whole = jnp.zeros_like(top)
    for p in range(peers):
        whole = whole + jnp.exp2(arrived[p] - top)
    level = top + jnp.log2(whole)
    for p in range(peers):
        out[p] = level


def turn_kernel(t, out):
    def turn(c, carry):
        at = pl.ds(pl.multiple_of(c * HALF, HALF), HALF)
        out[at, :] = jnp.transpose(t[:, at])
        return carry

    lax.fori_loop(0, t.shape[1] // HALF, turn, 0, unroll=4)


def moments_kernel(peers, stored, pairs, out, square):
    total = jnp.zeros((2 * stored, 2 * stored), F32)
    for p in range(peers):
        rows = pairs[p, : 2 * stored, :]
        total = total + nt(rows, rows, lax.Precision.HIGHEST)
    square[...] = jnp.zeros(square.shape, F32)
    square[:, : 2 * stored] = total
    lane = lax.broadcasted_iota(jnp.int32, (1, HALF), 1)
    line = jnp.zeros((1, HALF), F32)
    for k in range(stored):
        for row, place in ((k, cross_lane(k, k)), (stored + k, slope_lane(k, k))):
            kept = (lane >= stored + k) & (lane < 2 * stored)
            part = jnp.where(kept, square[row : row + 1, :], 0.0)
            line = line + pltpu.roll(part, (place - stored - k) % HALF, 1)
    out[...] = line


def row_kernel(
    blocks, own_blocks, ratio, peers, src, tgt, total, x, t, pot, level, pairs, out, acc
):
    acc[...] = jnp.zeros(acc.shape, F32)
    live = total[0]

    def turn(step, carry):
        found = []
        for u in range(UNROLL):
            b_all = src[step * UNROLL + u]
            t_all = tgt[step * UNROLL + u]
            b = jnp.minimum(b_all, blocks - 1)
            tb = jnp.minimum(t_all, own_blocks - 1)
            rows = x[b]
            lines = [pot[pl.ds(2 * b + h, 1), :] * SCALE for h in range(2)]
            line = jnp.concatenate(lines, axis=1)
            parts = None
            for h in range(2):
                cols = t[pl.ds(pl.multiple_of(tb * BLOCK + h * HALF, HALF), HALF), :]
                log_line = level[
                    lax.shift_right_logical(tb, 1), pl.ds(lax.rem(tb, 2) * 2 + h, 1), :
                ]
                shift = jnp.transpose(jnp.broadcast_to(log_line, (HALF, HALF)))
                s = nt(cols, rows) * SCALE + line
                e = jnp.exp2(s - jnp.concatenate([shift, shift], axis=1))
                part = jnp.sum(e.reshape(HALF // 8, 8, BLOCK), axis=0)
                parts = part if parts is None else parts + part
            found.append((b_all, parts))
        for b_all, parts in found:
            at = pl.ds(pl.multiple_of(b_all * 8, 8), 8)
            acc[at, :] = acc[at, :] + parts
        return carry

    lax.fori_loop(0, (live + UNROLL - 1) // UNROLL, turn, 0)

    rows_kept = pairs.shape[1] // 2
    lane = lax.broadcasted_iota(jnp.int32, (rows_kept, HALF), 1)
    row = lax.broadcasted_iota(jnp.int32, (rows_kept, HALF), 0)
    dots = jnp.zeros((rows_kept, HALF), F32)
    for p in range(blocks // 2):
        for half in range(2):
            at = pl.ds((2 * p + half) * 8, 8)
            part = 1.0 / peers - ratio * jnp.sum(acc[at, :], axis=0, keepdims=True)
            for h in range(2):
                q = 2 * half + h
                line = part[:, h * HALF : (h + 1) * HALF]
                out[p, q : q + 1, :] = line
                dots = dots + pairs[p, :rows_kept, q * HALF : (q + 1) * HALF] * line
    spread = jnp.where(lane == row, jnp.sum(dots, axis=1, keepdims=True), 0.0)
    value = jnp.sum(spread, axis=0, keepdims=True)
    for p in range(blocks // 2):
        out[p, 4:5, :] = value


def gradient_kernel(peers, src_size, arrived, moments, gradient, dots):
    whole = arrived[0]
    for p in range(1, peers):
        whole = whole + arrived[p]
    gradient[...] = whole[:4]
    value = whole[4:5] + moments[...]
    for p in range(src_size):
        dots[p] = value


def cross_lane(k, m):
    return 16 + 8 * k - k * (k - 1) // 2 + m - k


def slope_lane(k, m):
    k, m = min(k, m), max(k, m)
    return 52 + 8 * k - k * (k - 1) // 2 + m - k


def direction_kernel(peers, stored, arrived, gradient, steps, slopes, out):
    sums = arrived[0]
    for p in range(1, peers):
        sums = sums + arrived[p]

    def lane(c):
        return jnp.broadcast_to(sums[:, c : c + 1], (1, HALF))

    cross = [[lane(cross_lane(k, m)) if m >= k else None for m in range(stored)] for k in range(stored)]
    slope = [[lane(slope_lane(k, m)) for m in range(stored)] for k in range(stored)]
    rho = [1.0 / cross[k][k] for k in range(stored)]
    gamma = cross[stored - 1][stored - 1] / slope[stored - 1][stored - 1]
    left = [lane(k) for k in range(stored)]
    alpha = [None] * stored
    for k in reversed(range(stored)):
        alpha[k] = left[k] * rho[k]
        for j in range(k):
            left[j] = left[j] - alpha[k] * cross[j][k]
    left = [lane(stored + k) for k in range(stored)]
    for k in reversed(range(stored)):
        left = [left[j] - alpha[k] * slope[j][k] for j in range(stored)]
    left = [gamma * value for value in left]
    delta = [None] * stored
    for k in range(stored):
        delta[k] = alpha[k] - left[k] * rho[k]
        for j in range(k + 1, stored):
            left[j] = left[j] + delta[k] * cross[k][j]
    of_steps = jnp.concatenate([-delta[k] for k in range(stored)], axis=0)
    of_slopes = jnp.concatenate([gamma * alpha[k] for k in range(stored)], axis=0)
    for r in range(4):
        at = slice(r * HALF, (r + 1) * HALF)
        mix = jnp.sum(of_steps * steps[:, at] + of_slopes * slopes[:, at], axis=0, keepdims=True)
        out[r : r + 1, :] = mix - gamma * gradient[r : r + 1, :]


def per_device(sources, targets, potential, block_map, counts, step_history, slope_history):
    src_size, tgt_size = lax.axis_size(SRC), lax.axis_size(TGT)
    blocks = potential.shape[0] // BLOCK
    own_blocks = targets.shape[0] // BLOCK
    listed = block_map.shape[1]
    stored = step_history.shape[0]
    pieces = sources.shape[0] // BLOCK
    assert pieces == 2

    packed = jnp.concatenate([sources[:BLOCK], sources[BLOCK:]], axis=1)
    mine = share(packed, TGT[0])
    core = lax.axis_index(TGT[1])
    ttt = targets.T
    t = jnp.concatenate([ttt, ttt], axis=0)
    pot = potential.reshape(-1, HALF)
    lane = jnp.arange(HALF, dtype=jnp.int32)[None, :] // 64
    mask_row = jnp.arange(32, dtype=jnp.int32)[:, None] // 16
    mask = (lane == mask_row).astype(jnp.bfloat16)

    rank = jnp.stack([lax.axis_index(TGT), core]).astype(jnp.int32)
    slots = blocks * listed + UNROLL
    src, tgt, total = call(
        functools.partial(listing_kernel, blocks, own_blocks),
        (sds((slots,), jnp.int32), sds((slots,), jnp.int32), sds((1,), jnp.int32)),
        [SMEM] * 3,
        [SMEM] * 3,
    )(rank, block_map, counts)

    turned = call(turn_kernel, sds((targets.shape[0], HALF), jnp.bfloat16), [VMEM], VMEM)(t)
    other = lax.ppermute(mine, TGT[1], [(0, 1), (1, 0)])
    mine, other, t, turned = lax.optimization_barrier((mine, other, t, turned))
    history = jnp.concatenate([step_history, slope_history] * 2, axis=0)
    pairs = lax.all_gather(history, TGT)

    levels, x = call(
        functools.partial(column_kernel, blocks, own_blocks),
        (sds((src_size, 4, HALF)), sds((blocks, BLOCK, HALF), jnp.bfloat16)),
        [SMEM] * 4 + [VMEM] * 5,
        [VMEM] * 2,
        [pltpu.VMEM((8 * own_blocks + 8, BLOCK), F32)] * 2,
        pl.CostEstimate(flops=10**10, bytes_accessed=2 * 10**7, transcendentals=4 * 10**6),
    )(rank, src, tgt, total, mine, other, t, pot, mask)

    arrived = swap(levels, SRC)

    level = call(
        functools.partial(combine_kernel, src_size),
        sds((src_size, 4, HALF)),
        [VMEM],
        VMEM,
    )(arrived)
    level = swap(level, SRC)
    target_potential = (-entropy * LN2) * level.reshape(-1)

    moments = call(
        functools.partial(moments_kernel, tgt_size, stored),
        sds((1, HALF)),
        [VMEM],
        VMEM,
        [pltpu.VMEM((2 * stored, HALF), F32)],
    )(pairs)

    ratio = blocks * src_size / (own_blocks * tgt_size)
    parts = call(
        functools.partial(row_kernel, blocks, own_blocks, ratio, tgt_size),
        sds((tgt_size, 8, HALF)),
        [SMEM] * 3 + [VMEM] * 5,
        VMEM,
        [pltpu.VMEM((8 * blocks + 8, BLOCK), F32)],
        pl.CostEstimate(flops=10**10, bytes_accessed=2 * 10**7, transcendentals=4 * 10**6),
    )(src, tgt, total, x, turned, pot, level, pairs)

    gradient, dots = call(
        functools.partial(gradient_kernel, tgt_size, src_size),
        (sds((4, HALF)), sds((src_size, 1, HALF))),
        [VMEM] * 2,
        [VMEM] * 2,
    )(swap(parts, TGT), moments)
    direction = call(
        functools.partial(direction_kernel, src_size, stored), sds((4, HALF)), [VMEM] * 4, VMEM
    )(swap(dots, SRC), gradient, step_history, slope_history)
    return (gradient.reshape(-1), direction.reshape(-1), target_potential)


def solution(mesh):
    split = Mesh(mesh.devices.reshape(4, 8, 8, 2), ("src_0", "src_1", "tgt_0", "tgt_1"))
    in_specs = (
        P(SRC_TGT, None),
        P(TGT, None),
        P(SRC),
        P(SRC, None),
        P(SRC),
        P(None, SRC_TGT),
        P(None, SRC_TGT),
    )
    out_specs = (P(SRC_TGT), P(SRC_TGT), P(TGT))
    return jax.shard_map(
        per_device, mesh=split, in_specs=in_specs, out_specs=out_specs, check_vma=False
    )
```

```python
import functools

import jax
import jax.numpy as jnp
from jax import lax
from jax.experimental import pallas as pl
from jax.experimental.pallas import tpu as pltpu
from jax.sharding import Mesh
from jax.sharding import PartitionSpec as P

BLOCK = 256
HALF = 128
TGT = ("tgt_0", "tgt_1")
SRC = ("src_0", "src_1")
SRC_TGT = ("src_0", "src_1", "tgt_0", "tgt_1")
NEG = -1e30
LOG2E = 1.4426950408889634
LN2 = 0.6931471805599453
entropy = 0.5
SCALE = LOG2E / entropy
UNROLL = 8
WIDE = 64
F32 = jnp.float32

VMEM = pl.BlockSpec(memory_space=pltpu.VMEM)
SMEM = pl.BlockSpec(memory_space=pltpu.SMEM)


def call(body, out_shape, ins, outs, scratch=(), cost=None):
    return pl.pallas_call(
        body,
        out_shape=out_shape,
        in_specs=ins,
        out_specs=outs,
        scratch_shapes=list(scratch),
        cost_estimate=cost,
        compiler_params=pltpu.CompilerParams(vmem_limit_bytes=24 * 2**20),
    )


def sds(shape, dtype=F32):
    return jax.ShapeDtypeStruct(shape, dtype)


def nn(a, b):
    return jnp.dot(a, b, preferred_element_type=F32)


def nt(a, b, precision=None):
    return lax.dot_general(
        a, b, (((1,), (1,)), ((), ())), precision=precision, preferred_element_type=F32
    )


def swap(x, axis):
    return lax.all_to_all(x, axis, 0, 0, tiled=True)


def share(x, axis):
    return swap(jnp.broadcast_to(x[None], (lax.axis_size(axis), *x.shape)), axis)


def listing_kernel(blocks, own_blocks, rank, block_map, counts, src, tgt, total):
    first = rank[0] * own_blocks

    def of_block(b, n):
        count = counts[b]
        for k in range(block_map.shape[1]):
            local = block_map[b, k] - first
            src[n] = b
            tgt[n] = local
            mine = (k < count) & (local >= 0) & (local < own_blocks)
            n = n + mine.astype(jnp.int32)
        return n

    n = lax.fori_loop(0, blocks, of_block, jnp.int32(0))
    total[0] = n
    for extra in range(UNROLL):
        src[n + extra] = blocks
        tgt[n + extra] = own_blocks


def split_three(value):
    high = value.astype(jnp.bfloat16).astype(F32)
    rest = value - high
    middle = rest.astype(jnp.bfloat16).astype(F32)
    return high, middle, rest - middle


def columns_kernel(pot, out):
    row = lax.broadcasted_iota(jnp.int32, (HALF, HALF), 0)
    ones = jnp.where((row >= WIDE + 3) & (row < WIDE + 6), 1.0, 0.0)

    def turn(c, carry):
        parts = split_three(pot[pl.ds(c, 1), :])
        tile = ones
        for k in range(3):
            tile = jnp.where(row == WIDE + k, parts[k], tile)
        at = pl.ds(pl.multiple_of(lax.rem(c, 2) * HALF, HALF), HALF)
        out[lax.shift_right_logical(c, 1), at, :] = jnp.transpose(tile).astype(jnp.bfloat16)
        return carry

    lax.fori_loop(0, pot.shape[0], turn, 0, unroll=4)


def lay_out(rank, mine, other, columns, x):
    core = rank[1]
    lane = lax.broadcasted_iota(jnp.int32, (BLOCK, HALF), 1)
    for arrived, side in ((mine, core), (other, 1 - core)):
        for y in range(arrived.shape[0]):
            piece = arrived[y]
            for half in range(2):
                b = 4 * y + 2 * side + half
                if half:
                    piece = jnp.concatenate([piece[:, WIDE:], piece[:, :WIDE]], axis=1)
                x[b] = jnp.where(lane < WIDE, piece, columns[b])


def target_columns(t, tb, h, extra):
    cols = t[:, pl.ds(pl.multiple_of(tb * BLOCK + h * HALF, HALF), HALF)]
    zeros = jnp.zeros((HALF - WIDE - 16, HALF), jnp.bfloat16)
    return jnp.concatenate([cols, extra.astype(jnp.bfloat16), zeros], axis=0)


def column_kernel(
    blocks, own_blocks, rank, src, tgt, total, mine, other, t, columns, out, x, peak, acc
):
    lay_out(rank, mine, other, columns, x)
    peak[...] = jnp.full(peak.shape, NEG, F32)
    acc[...] = jnp.zeros(acc.shape, F32)
    live = total[0]
    row = lax.broadcasted_iota(jnp.int32, (16, HALF), 0)
    extra = jnp.where(row < 3, 1.0, 0.0)

    def turn(step, carry):
        found = []
        for u in range(UNROLL):
            b_all = src[step * UNROLL + u]
            t_all = tgt[step * UNROLL + u]
            b = jnp.minimum(b_all, blocks - 1)
            tb = jnp.minimum(t_all, own_blocks - 1)
            rows = x[b]
            for h in range(2):
                s = nn(rows, target_columns(t, tb, h, extra)) * SCALE
                s = s.reshape(BLOCK // 8, 8, HALF)
                top = jnp.max(s, axis=0)
                part = jnp.sum(jnp.exp2(s - top[None]), axis=0)
                found.append((t_all, h, top, part))
        for t_all, h, top, part in found:
            at = (pl.ds(pl.multiple_of(t_all * 8, 8), 8), slice(h * HALF, (h + 1) * HALF))
            old = peak[at]
            new = jnp.maximum(old, top)
            acc[at] = acc[at] * jnp.exp2(old - new) + part * jnp.exp2(top - new)
            peak[at] = new
        return carry

    lax.fori_loop(0, (live + UNROLL - 1) // UNROLL, turn, 0)

    def finish(p, carry):
        for r in range(4):
            at = (
                pl.ds(pl.multiple_of((2 * p + r // 2) * 8, 8), 8),
                slice((r % 2) * HALF, (r % 2 + 1) * HALF),
            )
            tops = peak[at]
            top = jnp.max(tops, axis=0, keepdims=True)
            whole = jnp.sum(acc[at] * jnp.exp2(tops - top), axis=0, keepdims=True)
            level = jnp.where(whole > 0.0, top + jnp.log2(jnp.maximum(whole, 1e-38)), NEG)
            out[p, r : r + 1, :] = level
        return carry

    lax.fori_loop(0, own_blocks // 2, finish, 0, unroll=4)


def combine_kernel(peers, arrived, out):
    top = arrived[0]
    for p in range(1, peers):
        top = jnp.maximum(top, arrived[p])
    whole = jnp.zeros_like(top)
    for p in range(peers):
        whole = whole + jnp.exp2(arrived[p] - top)
    level = (-entropy * LN2) * (top + jnp.log2(whole))
    for p in range(peers):
        out[p] = level


def moments_kernel(peers, stored, pairs, out, square):
    total = jnp.zeros((2 * stored, 2 * stored), F32)
    for p in range(peers):
        rows = pairs[p, : 2 * stored, :]
        total = total + nt(rows, rows, lax.Precision.HIGHEST)
    square[...] = jnp.zeros(square.shape, F32)
    square[:, : 2 * stored] = total
    lane = lax.broadcasted_iota(jnp.int32, (1, HALF), 1)
    line = jnp.zeros((1, HALF), F32)
    for k in range(stored):
        for row, place in ((k, cross_lane(k, k)), (stored + k, slope_lane(k, k))):
            kept = (lane >= stored + k) & (lane < 2 * stored)
            part = jnp.where(kept, square[row : row + 1, :], 0.0)
            line = line + pltpu.roll(part, (place - stored - k) % HALF, 1)
    out[...] = line


def row_kernel(
    blocks, own_blocks, ratio, peers, src, tgt, total, x, t, level, pairs, out, acc, sums
):
    acc[...] = jnp.zeros(acc.shape, F32)
    live = total[0]
    row = lax.broadcasted_iota(jnp.int32, (16, HALF), 0)
    ones = jnp.where(row < 3, 1.0, 0.0)

    def turn(step, carry):
        found = []
        for u in range(UNROLL):
            b_all = src[step * UNROLL + u]
            t_all = tgt[step * UNROLL + u]
            b = jnp.minimum(b_all, blocks - 1)
            tb = jnp.minimum(t_all, own_blocks - 1)
            rows = x[b]
            parts = None
            for h in range(2):
                line = level[
                    lax.shift_right_logical(tb, 1), pl.ds(lax.rem(tb, 2) * 2 + h, 1), :
                ]
                extra = ones
                for k, part in enumerate(split_three(line)):
                    extra = jnp.where(row == 3 + k, part, extra)
                e = jnp.exp2(nn(rows, target_columns(t, tb, h, extra)) * SCALE)
                parts = e if parts is None else parts + e
            found.append((b_all, parts))
        for b_all, parts in found:
            acc[b_all] = acc[b_all] + parts
        return carry

    lax.fori_loop(0, (live + UNROLL - 1) // UNROLL, turn, 0)

    def fold(b, carry):
        for h in range(2):
            turned = jnp.transpose(acc[b, h * HALF : (h + 1) * HALF, :])
            at = pl.ds(lax.rem(b, 2) * 2 + h, 1)
            sums[lax.shift_right_logical(b, 1), at, :] = jnp.sum(turned, axis=0, keepdims=True)
        return carry

    lax.fori_loop(0, blocks, fold, 0, unroll=4)

    rows_kept = pairs.shape[1] // 2
    lane = lax.broadcasted_iota(jnp.int32, (rows_kept, HALF), 1)
    row = lax.broadcasted_iota(jnp.int32, (rows_kept, HALF), 0)
    dots = jnp.zeros((rows_kept, HALF), F32)
    for p in range(blocks // 2):
        part = 1.0 / peers - ratio * sums[p]
        out[p, :4, :] = part
        for q in range(4):
            at = slice(q * HALF, (q + 1) * HALF)
            dots = dots + pairs[p, :rows_kept, at] * part[q : q + 1]
    spread = jnp.where(lane == row, jnp.sum(dots, axis=1, keepdims=True), 0.0)
    value = jnp.sum(spread, axis=0, keepdims=True)
    for p in range(blocks // 2):
        out[p, 4:5, :] = value


def gradient_kernel(peers, src_size, arrived, moments, gradient, dots):
    whole = arrived[0]
    for p in range(1, peers):
        whole = whole + arrived[p]
    gradient[...] = whole[:4]
    value = whole[4:5] + moments[...]
    for p in range(src_size):
        dots[p] = value


def cross_lane(k, m):
    return 16 + 8 * k - k * (k - 1) // 2 + m - k


def slope_lane(k, m):
    k, m = min(k, m), max(k, m)
    return 52 + 8 * k - k * (k - 1) // 2 + m - k


def direction_kernel(peers, stored, arrived, gradient, steps, slopes, out):
    sums = arrived[0]
    for p in range(1, peers):
        sums = sums + arrived[p]

    def lane(c):
        return jnp.broadcast_to(sums[:, c : c + 1], (1, HALF))

    cross = [[lane(cross_lane(k, m)) if m >= k else None for m in range(stored)] for k in range(stored)]
    slope = [[lane(slope_lane(k, m)) for m in range(stored)] for k in range(stored)]
    rho = [1.0 / cross[k][k] for k in range(stored)]
    gamma = cross[stored - 1][stored - 1] / slope[stored - 1][stored - 1]
    left = [lane(k) for k in range(stored)]
    alpha = [None] * stored
    for k in reversed(range(stored)):
        alpha[k] = left[k] * rho[k]
        for j in range(k):
            left[j] = left[j] - alpha[k] * cross[j][k]
    left = [lane(stored + k) for k in range(stored)]
    for k in reversed(range(stored)):
        left = [left[j] - alpha[k] * slope[j][k] for j in range(stored)]
    left = [gamma * value for value in left]
    delta = [None] * stored
    for k in range(stored):
        delta[k] = alpha[k] - left[k] * rho[k]
        for j in range(k + 1, stored):
            left[j] = left[j] + delta[k] * cross[k][j]
    of_steps = jnp.concatenate([-delta[k] for k in range(stored)], axis=0)
    of_slopes = jnp.concatenate([gamma * alpha[k] for k in range(stored)], axis=0)
    for r in range(4):
        at = slice(r * HALF, (r + 1) * HALF)
        mix = jnp.sum(of_steps * steps[:, at] + of_slopes * slopes[:, at], axis=0, keepdims=True)
        out[r : r + 1, :] = mix - gamma * gradient[r : r + 1, :]


def per_device(sources, targets, potential, block_map, counts, step_history, slope_history):
    src_size, tgt_size = lax.axis_size(SRC), lax.axis_size(TGT)
    blocks = potential.shape[0] // BLOCK
    own_blocks = targets.shape[0] // BLOCK
    listed = block_map.shape[1]
    stored = step_history.shape[0]
    pieces = sources.shape[0] // BLOCK
    assert pieces == 2

    packed = jnp.concatenate([sources[:BLOCK], sources[BLOCK:]], axis=1)
    mine = share(packed, TGT[0])
    core = lax.axis_index(TGT[1])
    t = targets.T
    columns = call(
        columns_kernel, sds((blocks, BLOCK, HALF), jnp.bfloat16), [VMEM], VMEM
    )(potential.reshape(-1, HALF))

    rank = jnp.stack([lax.axis_index(TGT), core]).astype(jnp.int32)
    slots = blocks * listed + UNROLL
    src, tgt, total = call(
        functools.partial(listing_kernel, blocks, own_blocks),
        (sds((slots,), jnp.int32), sds((slots,), jnp.int32), sds((1,), jnp.int32)),
        [SMEM] * 3,
        [SMEM] * 3,
    )(rank, block_map, counts)

    mine, columns, src, tgt, total = lax.optimization_barrier((mine, columns, src, tgt, total))
    other = lax.ppermute(mine, TGT[1], [(0, 1), (1, 0)])
    history = jnp.concatenate([step_history, slope_history] * 2, axis=0)
    pairs = lax.all_gather(history, TGT)

    levels, x = call(
        functools.partial(column_kernel, blocks, own_blocks),
        (sds((src_size, 4, HALF)), sds((blocks, BLOCK, HALF), jnp.bfloat16)),
        [SMEM] * 4 + [VMEM] * 4,
        [VMEM] * 2,
        [pltpu.VMEM((8 * own_blocks + 8, BLOCK), F32)] * 2,
        pl.CostEstimate(flops=10**10, bytes_accessed=2 * 10**7, transcendentals=4 * 10**6),
    )(rank, src, tgt, total, mine, other, t, columns)

    arrived = swap(levels, SRC)

    level = call(
        functools.partial(combine_kernel, src_size),
        sds((src_size, 4, HALF)),
        [VMEM],
        VMEM,
    )(arrived)
    level = swap(level, SRC)
    target_potential = level.reshape(-1)

    moments = call(
        functools.partial(moments_kernel, tgt_size, stored),
        sds((1, HALF)),
        [VMEM],
        VMEM,
        [pltpu.VMEM((2 * stored, HALF), F32)],
    )(pairs)

    ratio = blocks * src_size / (own_blocks * tgt_size)
    parts = call(
        functools.partial(row_kernel, blocks, own_blocks, ratio, tgt_size),
        sds((tgt_size, 8, HALF)),
        [SMEM] * 3 + [VMEM] * 4,
        VMEM,
        [pltpu.VMEM((blocks + 1, BLOCK, HALF), F32), pltpu.VMEM((tgt_size, 4, HALF), F32)],
        pl.CostEstimate(flops=10**10, bytes_accessed=2 * 10**7, transcendentals=4 * 10**6),
    )(src, tgt, total, x, t, level, pairs)

    gradient, dots = call(
        functools.partial(gradient_kernel, tgt_size, src_size),
        (sds((4, HALF)), sds((src_size, 1, HALF))),
        [VMEM] * 2,
        [VMEM] * 2,
    )(swap(parts, TGT), moments)
    direction = call(
        functools.partial(direction_kernel, src_size, stored), sds((4, HALF)), [VMEM] * 4, VMEM
    )(swap(dots, SRC), gradient, step_history, slope_history)
    return (gradient.reshape(-1), direction.reshape(-1), target_potential)


def solution(mesh):
    split = Mesh(mesh.devices.reshape(4, 8, 8, 2), ("src_0", "src_1", "tgt_0", "tgt_1"))
    in_specs = (
        P(SRC_TGT, None),
        P(TGT, None),
        P(SRC),
        P(SRC, None),
        P(SRC),
        P(None, SRC_TGT),
        P(None, SRC_TGT),
    )
    out_specs = (P(SRC_TGT), P(SRC_TGT), P(TGT))
    return jax.shard_map(
        per_device, mesh=split, in_specs=in_specs, out_specs=out_specs, check_vma=False
    )
```

```python
import functools

import jax
import jax.numpy as jnp
from jax import lax
from jax.experimental import pallas as pl
from jax.experimental.pallas import tpu as pltpu
from jax.sharding import Mesh
from jax.sharding import PartitionSpec as P

BLOCK = 256
HALF = 128
TGT = ("tgt_0", "tgt_1")
SRC = ("src_0", "src_1")
SRC_TGT = ("src_0", "src_1", "tgt_0", "tgt_1")
NEG = -1e30
LOG2E = 1.4426950408889634
LN2 = 0.6931471805599453
entropy = 0.5
SCALE = LOG2E / entropy
UNROLL = 8
PLACE = 1 << 16
WIDE = 64
F32 = jnp.float32

VMEM = pl.BlockSpec(memory_space=pltpu.VMEM)
SMEM = pl.BlockSpec(memory_space=pltpu.SMEM)


COST = pl.CostEstimate(flops=10**10, bytes_accessed=10**6, transcendentals=0)


def call(body, out_shape, ins, outs, scratch=(), cost=None):
    return pl.pallas_call(
        body,
        out_shape=out_shape,
        in_specs=ins,
        out_specs=outs,
        scratch_shapes=list(scratch),
        cost_estimate=cost,
        compiler_params=pltpu.CompilerParams(vmem_limit_bytes=24 * 2**20),
    )


def sds(shape, dtype=F32):
    return jax.ShapeDtypeStruct(shape, dtype)


def nn(a, b):
    return jnp.dot(a, b, preferred_element_type=F32)


def nt(a, b, precision=None):
    return lax.dot_general(
        a, b, (((1,), (1,)), ((), ())), precision=precision, preferred_element_type=F32
    )


def swap(x, axis):
    return lax.all_to_all(x, axis, 0, 0, tiled=True)


def share(x, axis):
    return swap(jnp.broadcast_to(x[None], (lax.axis_size(axis), *x.shape)), axis)


def listing_kernel(blocks, own_blocks, rank, block_map, counts, pairs, total):
    first = rank[0] * own_blocks
    core = rank[1]

    def of_block(b, n):
        count = counts[b]
        far = (lax.rem(lax.shift_right_logical(b, 1), 2) != core).astype(jnp.int32)
        place = far * (blocks // 2) + 2 * lax.shift_right_logical(b, 2) + lax.rem(b, 2)
        for k in range(block_map.shape[1]):
            local = block_map[b, k] - first
            pairs[n] = place * PLACE + local
            mine = (k < count) & (local >= 0) & (local < own_blocks)
            n = n + mine.astype(jnp.int32)
        return n

    n = lax.fori_loop(0, blocks, of_block, jnp.int32(0))
    total[0] = n
    for extra in range(UNROLL):
        pairs[n + extra] = blocks * PLACE + own_blocks


def split_three(value):
    high = value.astype(jnp.bfloat16).astype(F32)
    rest = value - high
    middle = rest.astype(jnp.bfloat16).astype(F32)
    return high, middle, rest - middle


def columns_kernel(rank, pot, out, tile):
    core = rank[1]
    tile[...] = jnp.zeros(tile.shape, F32)
    ys = pot.shape[0] // 8
    for h in range(2):
        for far in range(2):
            for y in range(ys):
                for half in range(2):
                    side = 1 - core if far else core
                    parts = split_three(pot[pl.ds(8 * y + 4 * side + 2 * half + h, 1), :])
                    for k in range(3):
                        at = 4 * (2 * ys * far + 2 * y + half) + k
                        tile[at : at + 1, :] = parts[k]
        out[h * HALF : (h + 1) * HALF, :] = jnp.transpose(tile[...]).astype(jnp.bfloat16)


def turned(value, by):
    return jnp.concatenate([value[:, by:], value[:, :by]], axis=1) if by % HALF else value


def lay_out(mine, other, columns, x):
    lane = lax.broadcasted_iota(jnp.int32, (BLOCK, HALF), 1)
    ones = jnp.where((lane >= WIDE + 3) & (lane < WIDE + 6), 1.0, 0.0).astype(jnp.bfloat16)
    own = columns[...]
    place = 0
    for arrived in (mine, other):
        for y in range(arrived.shape[0]):
            piece = arrived[y]
            for half in range(2):
                parts = turned(own, (4 * place - WIDE) % HALF)
                rest = jnp.where((lane >= WIDE) & (lane < WIDE + 3), parts, ones)
                x[place] = jnp.where(lane < WIDE, turned(piece, WIDE * half), rest)
                place += 1


def target_columns(t, tb, h, extra):
    cols = t[:, pl.ds(pl.multiple_of(tb * BLOCK + h * HALF, HALF), HALF)]
    zeros = jnp.zeros((HALF - WIDE - 16, HALF), jnp.bfloat16)
    return jnp.concatenate([cols, extra.astype(jnp.bfloat16), zeros], axis=0)


def column_kernel(
    blocks, own_blocks, listed, total, mine, other, t, columns, out, x, peak, acc
):
    lay_out(mine, other, columns, x)
    peak[...] = jnp.full(peak.shape, NEG, F32)
    acc[...] = jnp.zeros(acc.shape, F32)
    live = total[0]
    row = lax.broadcasted_iota(jnp.int32, (16, HALF), 0)
    extra = jnp.where(row < 3, 1.0, 0.0)

    def turn(step, carry):
        found = []
        for u in range(UNROLL):
            pair = listed[step * UNROLL + u]
            b_all = lax.shift_right_logical(pair, 16)
            t_all = lax.bitwise_and(pair, PLACE - 1)
            b = jnp.minimum(b_all, blocks - 1)
            tb = jnp.minimum(t_all, own_blocks - 1)
            rows = x[b]
            for h in range(2):
                s = nn(rows, target_columns(t, tb, h, extra)) * SCALE
                s = s.reshape(BLOCK // 8, 8, HALF)
                top = jnp.max(s, axis=0)
                part = jnp.sum(jnp.exp2(s - top[None]), axis=0)
                found.append((t_all, h, top, part))
        for t_all, h, top, part in found:
            at = (pl.ds(pl.multiple_of(t_all * 8, 8), 8), slice(h * HALF, (h + 1) * HALF))
            old = peak[at]
            new = jnp.maximum(old, top)
            acc[at] = acc[at] * jnp.exp2(old - new) + part * jnp.exp2(top - new)
            peak[at] = new
        return carry

    lax.fori_loop(0, (live + UNROLL - 1) // UNROLL, turn, 0)

    def finish(p, carry):
        for r in range(4):
            at = (
                pl.ds(pl.multiple_of((2 * p + r // 2) * 8, 8), 8),
                slice((r % 2) * HALF, (r % 2 + 1) * HALF),
            )
            tops = peak[at]
            top = jnp.max(tops, axis=0, keepdims=True)
            whole = jnp.sum(acc[at] * jnp.exp2(tops - top), axis=0, keepdims=True)
            level = jnp.where(whole > 0.0, top + jnp.log2(jnp.maximum(whole, 1e-38)), NEG)
            out[p, r : r + 1, :] = level
        return carry

    lax.fori_loop(0, own_blocks // 2, finish, 0, unroll=4)


def combine_kernel(peers, arrived, out):
    top = arrived[0]
    for p in range(1, peers):
        top = jnp.maximum(top, arrived[p])
    whole = jnp.zeros_like(top)
    for p in range(peers):
        whole = whole + jnp.exp2(arrived[p] - top)
    level = top + jnp.log2(whole)
    for p in range(peers):
        out[p] = level


def moments_kernel(stored, near, far, out, square):
    total = jnp.zeros((2 * stored, 2 * stored), F32)
    for pairs in (near, far):
        for p in range(pairs.shape[0]):
            total = total + nt(pairs[p], pairs[p], lax.Precision.HIGHEST)
    square[...] = jnp.zeros(square.shape, F32)
    square[:, : 2 * stored] = total
    lane = lax.broadcasted_iota(jnp.int32, (1, HALF), 1)
    line = jnp.zeros((1, HALF), F32)
    for k in range(stored):
        for row, place in ((k, cross_lane(k, k)), (stored + k, slope_lane(k, k))):
            kept = (lane >= stored + k) & (lane < 2 * stored)
            part = jnp.where(kept, square[row : row + 1, :], 0.0)
            line = line + pltpu.roll(part, (place - stored - k) % HALF, 1)
    out[...] = line


def row_kernel(
    blocks,
    own_blocks,
    ratio,
    peers,
    rank,
    listed,
    total,
    mine,
    other,
    t,
    columns,
    level,
    near,
    far,
    out,
    x,
    acc,
    sums,
):
    lay_out(mine, other, columns, x)
    acc[...] = jnp.zeros(acc.shape, F32)
    live = total[0]
    row = lax.broadcasted_iota(jnp.int32, (16, HALF), 0)
    ones = jnp.where(row < 3, 1.0, 0.0)

    def turn(step, carry):
        found = []
        for u in range(UNROLL):
            pair = listed[step * UNROLL + u]
            b_all = lax.shift_right_logical(pair, 16)
            t_all = lax.bitwise_and(pair, PLACE - 1)
            b = jnp.minimum(b_all, blocks - 1)
            tb = jnp.minimum(t_all, own_blocks - 1)
            rows = x[b]
            parts = None
            for h in range(2):
                line = level[
                    lax.shift_right_logical(tb, 1), pl.ds(lax.rem(tb, 2) * 2 + h, 1), :
                ]
                extra = ones
                for k, part in enumerate(split_three((-entropy * LN2) * line)):
                    extra = jnp.where(row == 3 + k, part, extra)
                e = jnp.exp2(nn(rows, target_columns(t, tb, h, extra)) * SCALE)
                parts = e if parts is None else parts + e
            found.append((b_all, parts))
        for b_all, parts in found:
            acc[b_all] = acc[b_all] + parts
        return carry

    lax.fori_loop(0, (live + UNROLL - 1) // UNROLL, turn, 0)

    def fold(b, carry):
        for h in range(2):
            turned = jnp.transpose(acc[b, h * HALF : (h + 1) * HALF, :])
            at = pl.ds(lax.rem(b, 2) * 2 + h, 1)
            sums[lax.shift_right_logical(b, 1), at, :] = jnp.sum(turned, axis=0, keepdims=True)
        return carry

    lax.fori_loop(0, blocks, fold, 0, unroll=4)

    rows_kept = near.shape[1]
    lane = lax.broadcasted_iota(jnp.int32, (rows_kept, HALF), 1)
    row = lax.broadcasted_iota(jnp.int32, (rows_kept, HALF), 0)
    dots = jnp.zeros((rows_kept, HALF), F32)
    core = rank[1]
    place = 0
    for pairs, side in ((near, core), (far, 1 - core)):
        for y in range(pairs.shape[0]):
            part = 1.0 / peers - ratio * sums[place]
            place += 1
            out[2 * y + side, :4, :] = part
            for q in range(4):
                at = slice(q * HALF, (q + 1) * HALF)
                dots = dots + pairs[y, :, at] * part[q : q + 1]
    spread = jnp.where(lane == row, jnp.sum(dots, axis=1, keepdims=True), 0.0)
    value = jnp.sum(spread, axis=0, keepdims=True)
    for p in range(blocks // 2):
        out[p, 4:5, :] = value


def gradient_kernel(peers, src_size, arrived, moments, gradient, again, dots):
    whole = arrived[0]
    for p in range(1, peers):
        whole = whole + arrived[p]
    gradient[...] = whole[:4]
    again[...] = whole[:4]
    value = whole[4:5] + moments[...]
    for p in range(src_size):
        dots[p] = value


def cross_lane(k, m):
    return 16 + 8 * k - k * (k - 1) // 2 + m - k


def slope_lane(k, m):
    k, m = min(k, m), max(k, m)
    return 52 + 8 * k - k * (k - 1) // 2 + m - k


def direction_kernel(peers, stored, arrived, gradient, steps, slopes, out):
    sums = arrived[0]
    for p in range(1, peers):
        sums = sums + arrived[p]

    def lane(c):
        return jnp.broadcast_to(sums[:, c : c + 1], (1, HALF))

    cross = [[lane(cross_lane(k, m)) if m >= k else None for m in range(stored)] for k in range(stored)]
    slope = [[lane(slope_lane(k, m)) for m in range(stored)] for k in range(stored)]
    rho = [1.0 / cross[k][k] for k in range(stored)]
    gamma = cross[stored - 1][stored - 1] / slope[stored - 1][stored - 1]
    left = [lane(k) for k in range(stored)]
    alpha = [None] * stored
    for k in reversed(range(stored)):
        alpha[k] = left[k] * rho[k]
        for j in range(k):
            left[j] = left[j] - alpha[k] * cross[j][k]
    left = [lane(stored + k) for k in range(stored)]
    for k in reversed(range(stored)):
        left = [left[j] - alpha[k] * slope[j][k] for j in range(stored)]
    left = [gamma * value for value in left]
    delta = [None] * stored
    for k in range(stored):
        delta[k] = alpha[k] - left[k] * rho[k]
        for j in range(k + 1, stored):
            left[j] = left[j] + delta[k] * cross[k][j]
    of_steps = jnp.concatenate([-delta[k] for k in range(stored)], axis=0)
    of_slopes = jnp.concatenate([gamma * alpha[k] for k in range(stored)], axis=0)
    for r in range(4):
        at = slice(r * HALF, (r + 1) * HALF)
        mix = jnp.sum(of_steps * steps[:, at] + of_slopes * slopes[:, at], axis=0, keepdims=True)
        out[r : r + 1, :] = mix - gamma * gradient[r : r + 1, :]


def per_device(sources, targets, potential, block_map, counts, step_history, slope_history):
    src_size, tgt_size = lax.axis_size(SRC), lax.axis_size(TGT)
    blocks = potential.shape[0] // BLOCK
    own_blocks = targets.shape[0] // BLOCK
    listed = block_map.shape[1]
    stored = step_history.shape[0]
    pieces = sources.shape[0] // BLOCK
    assert pieces == 2

    packed = jnp.concatenate([sources[:BLOCK], sources[BLOCK:]], axis=1)
    mine = share(packed, TGT[0])
    core = lax.axis_index(TGT[1])
    t = targets.T
    rank = jnp.stack([lax.axis_index(TGT), core]).astype(jnp.int32)
    columns = call(
        columns_kernel,
        sds((BLOCK, HALF), jnp.bfloat16),
        [SMEM, VMEM],
        VMEM,
        [pltpu.VMEM((HALF, HALF), F32)],
    )(rank, potential.reshape(-1, HALF))
    slots = blocks * listed + UNROLL
    pairs, total = call(
        functools.partial(listing_kernel, blocks, own_blocks),
        (sds((slots,), jnp.int32), sds((1,), jnp.int32)),
        [SMEM] * 3,
        [SMEM] * 2,
    )(rank, block_map, counts)

    mine, columns, pairs, total = lax.optimization_barrier((mine, columns, pairs, total))
    other = lax.ppermute(mine, TGT[1], [(0, 1), (1, 0)])
    history = jnp.concatenate([step_history, slope_history], axis=0)
    mine, history = lax.optimization_barrier((mine, history))
    near = share(history, TGT[0])

    rows = pltpu.VMEM((blocks, BLOCK, HALF), jnp.bfloat16)
    levels = call(
        functools.partial(column_kernel, blocks, own_blocks),
        sds((src_size, 4, HALF)),
        [SMEM] * 2 + [VMEM] * 4,
        VMEM,
        [rows] + [pltpu.VMEM((8 * own_blocks + 8, BLOCK), F32)] * 2,
        COST,
    )(pairs, total, mine, other, t, columns)

    levels, near = lax.optimization_barrier((levels, near))
    arrived = swap(levels, SRC)
    far = lax.ppermute(near, TGT[1], [(0, 1), (1, 0)])

    level = call(
        functools.partial(combine_kernel, src_size),
        sds((src_size, 4, HALF)),
        [VMEM],
        VMEM,
    )(arrived)
    level = swap(level, SRC)
    target_potential = (-entropy * LN2) * level.reshape(-1)

    moments = call(
        functools.partial(moments_kernel, stored),
        sds((1, HALF)),
        [VMEM] * 2,
        VMEM,
        [pltpu.VMEM((2 * stored, HALF), F32)],
    )(near, far)

    ratio = blocks * src_size / (own_blocks * tgt_size)
    parts = call(
        functools.partial(row_kernel, blocks, own_blocks, ratio, tgt_size),
        sds((tgt_size, 8, HALF)),
        [SMEM] * 3 + [VMEM] * 7,
        VMEM,
        [
            rows,
            pltpu.VMEM((blocks + 1, BLOCK, HALF), F32),
            pltpu.VMEM((tgt_size, 4, HALF), F32),
        ],
        COST,
    )(rank, pairs, total, mine, other, t, columns, level, near, far)

    gradient, again, dots = call(
        functools.partial(gradient_kernel, tgt_size, src_size),
        (sds((4, HALF)), sds((4, HALF)), sds((src_size, 1, HALF))),
        [VMEM] * 2,
        [VMEM] * 3,
    )(swap(parts, TGT), moments)
    direction = call(
        functools.partial(direction_kernel, src_size, stored), sds((4, HALF)), [VMEM] * 4, VMEM
    )(swap(dots, SRC), again, step_history, slope_history)
    return (gradient.reshape(-1), direction.reshape(-1), target_potential)


def solution(mesh):
    split = Mesh(mesh.devices.reshape(4, 8, 8, 2), ("src_0", "src_1", "tgt_0", "tgt_1"))
    in_specs = (
        P(SRC_TGT, None),
        P(TGT, None),
        P(SRC),
        P(SRC, None),
        P(SRC),
        P(None, SRC_TGT),
        P(None, SRC_TGT),
    )
    out_specs = (P(SRC_TGT), P(SRC_TGT), P(TGT))
    return jax.shard_map(
        per_device, mesh=split, in_specs=in_specs, out_specs=out_specs, check_vma=False
    )
```

```python
import functools

import jax
import jax.numpy as jnp
from jax import lax
from jax.experimental import pallas as pl
from jax.experimental.pallas import tpu as pltpu
from jax.sharding import Mesh
from jax.sharding import PartitionSpec as P

BLOCK = 256
HALF = 128
TGT = ("tgt_0", "tgt_1")
SRC = ("src_0", "src_1")
SRC_TGT = ("src_0", "src_1", "tgt_0", "tgt_1")
NEG = -1e30
LOG2E = 1.4426950408889634
LN2 = 0.6931471805599453
entropy = 0.5
SCALE = LOG2E / entropy
UNROLL = 8
PLACE = 1 << 16
WIDE = 64
F32 = jnp.float32

VMEM = pl.BlockSpec(memory_space=pltpu.VMEM)
SMEM = pl.BlockSpec(memory_space=pltpu.SMEM)


COST = pl.CostEstimate(flops=10**10, bytes_accessed=10**6, transcendentals=0)


def call(body, out_shape, ins, outs, scratch=(), cost=None):
    return pl.pallas_call(
        body,
        out_shape=out_shape,
        in_specs=ins,
        out_specs=outs,
        scratch_shapes=list(scratch),
        cost_estimate=cost,
        compiler_params=pltpu.CompilerParams(vmem_limit_bytes=24 * 2**20),
    )


def sds(shape, dtype=F32):
    return jax.ShapeDtypeStruct(shape, dtype)


def nn(a, b):
    return jnp.dot(a, b, preferred_element_type=F32)


def nt(a, b, precision=None):
    return lax.dot_general(
        a, b, (((1,), (1,)), ((), ())), precision=precision, preferred_element_type=F32
    )


def swap(x, axis):
    return lax.all_to_all(x, axis, 0, 0, tiled=True)


def share(x, axis):
    return swap(jnp.broadcast_to(x[None], (lax.axis_size(axis), *x.shape)), axis)


def listing_kernel(blocks, own_blocks, rank, block_map, counts, pairs, total):
    first = rank[0] * own_blocks
    core = rank[1]

    def of_block(b, n):
        count = counts[b]
        far = (lax.rem(lax.shift_right_logical(b, 1), 2) != core).astype(jnp.int32)
        place = far * (blocks // 2) + 2 * lax.shift_right_logical(b, 2) + lax.rem(b, 2)
        for k in range(block_map.shape[1]):
            local = block_map[b, k] - first
            pairs[n] = place * PLACE + local
            mine = (k < count) & (local >= 0) & (local < own_blocks)
            n = n + mine.astype(jnp.int32)
        return n

    n = lax.fori_loop(0, blocks, of_block, jnp.int32(0))
    total[0] = n
    for extra in range(UNROLL):
        pairs[n + extra] = blocks * PLACE + own_blocks


def split_three(value):
    high = value.astype(jnp.bfloat16).astype(F32)
    rest = value - high
    middle = rest.astype(jnp.bfloat16).astype(F32)
    return high, middle, rest - middle


def columns_kernel(rank, pot, out, tile):
    core = rank[1]
    tile[...] = jnp.zeros(tile.shape, F32)
    ys = pot.shape[0] // 8
    for h in range(2):
        for far in range(2):
            for y in range(ys):
                for half in range(2):
                    side = 1 - core if far else core
                    parts = split_three(pot[pl.ds(8 * y + 4 * side + 2 * half + h, 1), :])
                    for k in range(3):
                        at = 4 * (2 * ys * far + 2 * y + half) + k
                        tile[at : at + 1, :] = parts[k]
        out[h * HALF : (h + 1) * HALF, :] = jnp.transpose(tile[...]).astype(jnp.bfloat16)


def turned(value, by):
    return jnp.concatenate([value[:, by:], value[:, :by]], axis=1) if by % HALF else value


def lay_out(mine, other, columns, x):
    lane = lax.broadcasted_iota(jnp.int32, (BLOCK, HALF), 1)
    ones = jnp.where((lane >= WIDE + 3) & (lane < WIDE + 6), 1.0, 0.0).astype(jnp.bfloat16)
    own = columns[...]
    place = 0
    for arrived in (mine, other):
        for y in range(arrived.shape[0]):
            piece = arrived[y]
            for half in range(2):
                parts = turned(own, (4 * place - WIDE) % HALF)
                rest = jnp.where((lane >= WIDE) & (lane < WIDE + 3), parts, ones)
                x[place] = jnp.where(lane < WIDE, turned(piece, WIDE * half), rest)
                place += 1


def target_columns(t, tb, h, extra):
    cols = t[:, pl.ds(pl.multiple_of(tb * BLOCK + h * HALF, HALF), HALF)]
    zeros = jnp.zeros((HALF - WIDE - 16, HALF), jnp.bfloat16)
    return jnp.concatenate([cols, extra.astype(jnp.bfloat16), zeros], axis=0)


def column_kernel(
    blocks, own_blocks, listed, total, mine, other, t, columns, out, x, peak, acc
):
    lay_out(mine, other, columns, x)
    peak[...] = jnp.full(peak.shape, NEG, F32)
    acc[...] = jnp.zeros(acc.shape, F32)
    live = total[0]
    row = lax.broadcasted_iota(jnp.int32, (16, HALF), 0)
    extra = jnp.where(row < 3, 1.0, 0.0)

    def turn(step, carry):
        found = []
        for u in range(UNROLL):
            pair = listed[step * UNROLL + u]
            b_all = lax.shift_right_logical(pair, 16)
            t_all = lax.bitwise_and(pair, PLACE - 1)
            b = jnp.minimum(b_all, blocks - 1)
            tb = jnp.minimum(t_all, own_blocks - 1)
            rows = x[b]
            for h in range(2):
                s = nn(rows, target_columns(t, tb, h, extra)) * SCALE
                s = s.reshape(BLOCK // 8, 8, HALF)
                top = jnp.max(s, axis=0)
                part = jnp.sum(jnp.exp2(s - top[None]), axis=0)
                found.append((t_all, h, top, part))
        for t_all, h, top, part in found:
            at = (pl.ds(pl.multiple_of(t_all * 8, 8), 8), slice(h * HALF, (h + 1) * HALF))
            old = peak[at]
            new = jnp.maximum(old, top)
            acc[at] = acc[at] * jnp.exp2(old - new) + part * jnp.exp2(top - new)
            peak[at] = new
        return carry

    lax.fori_loop(0, (live + UNROLL - 1) // UNROLL, turn, 0)

    def finish(p, carry):
        for r in range(4):
            at = (
                pl.ds(pl.multiple_of((2 * p + r // 2) * 8, 8), 8),
                slice((r % 2) * HALF, (r % 2 + 1) * HALF),
            )
            tops = peak[at]
            top = jnp.max(tops, axis=0, keepdims=True)
            whole = jnp.sum(acc[at] * jnp.exp2(tops - top), axis=0, keepdims=True)
            level = jnp.where(whole > 0.0, top + jnp.log2(jnp.maximum(whole, 1e-38)), NEG)
            out[p, r : r + 1, :] = level
        return carry

    lax.fori_loop(0, own_blocks // 2, finish, 0, unroll=4)


def combine_kernel(peers, arrived, out):
    top = arrived[0]
    for p in range(1, peers):
        top = jnp.maximum(top, arrived[p])
    whole = jnp.zeros_like(top)
    for p in range(peers):
        whole = whole + jnp.exp2(arrived[p] - top)
    level = top + jnp.log2(whole)
    for p in range(peers):
        out[p] = level


def moments_kernel(stored, history, out, square):
    total = nt(history[...], history[...], lax.Precision.HIGHEST)
    square[...] = jnp.zeros(square.shape, F32)
    square[:, : 2 * stored] = total
    lane = lax.broadcasted_iota(jnp.int32, (1, HALF), 1)
    line = jnp.zeros((1, HALF), F32)
    for k in range(stored):
        for row, place in ((k, cross_lane(k, k)), (stored + k, slope_lane(k, k))):
            kept = (lane >= stored + k) & (lane < 2 * stored)
            part = jnp.where(kept, square[row : row + 1, :], 0.0)
            line = line + pltpu.roll(part, (place - stored - k) % HALF, 1)
    out[...] = line


def row_kernel(
    blocks,
    own_blocks,
    rank,
    listed,
    total,
    mine,
    other,
    t,
    columns,
    level,
    out,
    x,
    acc,
    sums,
):
    lay_out(mine, other, columns, x)
    acc[...] = jnp.zeros(acc.shape, F32)
    live = total[0]
    row = lax.broadcasted_iota(jnp.int32, (16, HALF), 0)
    ones = jnp.where(row < 3, 1.0, 0.0)

    def turn(step, carry):
        found = []
        for u in range(UNROLL):
            pair = listed[step * UNROLL + u]
            b_all = lax.shift_right_logical(pair, 16)
            t_all = lax.bitwise_and(pair, PLACE - 1)
            b = jnp.minimum(b_all, blocks - 1)
            tb = jnp.minimum(t_all, own_blocks - 1)
            rows = x[b]
            parts = None
            for h in range(2):
                line = level[
                    lax.shift_right_logical(tb, 1), pl.ds(lax.rem(tb, 2) * 2 + h, 1), :
                ]
                extra = ones
                for k, part in enumerate(split_three((-entropy * LN2) * line)):
                    extra = jnp.where(row == 3 + k, part, extra)
                e = jnp.exp2(nn(rows, target_columns(t, tb, h, extra)) * SCALE)
                parts = e if parts is None else parts + e
            found.append((b_all, parts))
        for b_all, parts in found:
            acc[b_all] = acc[b_all] + parts
        return carry

    lax.fori_loop(0, (live + UNROLL - 1) // UNROLL, turn, 0)

    def fold(b, carry):
        for h in range(2):
            turned = jnp.transpose(acc[b, h * HALF : (h + 1) * HALF, :])
            at = pl.ds(lax.rem(b, 2) * 2 + h, 1)
            sums[lax.shift_right_logical(b, 1), at, :] = jnp.sum(turned, axis=0, keepdims=True)
        return carry

    lax.fori_loop(0, blocks, fold, 0, unroll=4)

    core = rank[1]
    place = 0
    for side in (core, 1 - core):
        for y in range(mine.shape[0]):
            out[2 * y + side] = sums[place]
            place += 1


def gradient_kernel(peers, ratio, arrived, history, moments, gradient, again, dots):
    whole = arrived[0]
    for p in range(1, peers):
        whole = whole + arrived[p]
    grad = 1.0 - ratio * whole
    gradient[...] = grad
    again[...] = grad
    rows_kept = history.shape[0]
    lane = lax.broadcasted_iota(jnp.int32, (rows_kept, HALF), 1)
    row = lax.broadcasted_iota(jnp.int32, (rows_kept, HALF), 0)
    total = jnp.zeros((rows_kept, HALF), F32)
    for q in range(4):
        total = total + history[:, q * HALF : (q + 1) * HALF] * grad[q : q + 1]
    spread = jnp.where(lane == row, jnp.sum(total, axis=1, keepdims=True), 0.0)
    value = jnp.sum(spread, axis=0, keepdims=True) + moments[...]
    for p in range(peers):
        dots[p] = value


def pass_on_kernel(arrived, out):
    value = arrived[0]
    for p in range(1, arrived.shape[0]):
        value = value + arrived[p]
    for p in range(out.shape[0]):
        out[p] = value


def cross_lane(k, m):
    return 16 + 8 * k - k * (k - 1) // 2 + m - k


def slope_lane(k, m):
    k, m = min(k, m), max(k, m)
    return 52 + 8 * k - k * (k - 1) // 2 + m - k


def direction_kernel(peers, stored, arrived, gradient, steps, slopes, out):
    sums = arrived[0]
    for p in range(1, peers):
        sums = sums + arrived[p]

    def lane(c):
        return jnp.broadcast_to(sums[:, c : c + 1], (1, HALF))

    cross = [[lane(cross_lane(k, m)) if m >= k else None for m in range(stored)] for k in range(stored)]
    slope = [[lane(slope_lane(k, m)) for m in range(stored)] for k in range(stored)]
    rho = [1.0 / cross[k][k] for k in range(stored)]
    gamma = cross[stored - 1][stored - 1] / slope[stored - 1][stored - 1]
    left = [lane(k) for k in range(stored)]
    alpha = [None] * stored
    for k in reversed(range(stored)):
        alpha[k] = left[k] * rho[k]
        for j in range(k):
            left[j] = left[j] - alpha[k] * cross[j][k]
    left = [lane(stored + k) for k in range(stored)]
    for k in reversed(range(stored)):
        left = [left[j] - alpha[k] * slope[j][k] for j in range(stored)]
    left = [gamma * value for value in left]
    delta = [None] * stored
    for k in range(stored):
        delta[k] = alpha[k] - left[k] * rho[k]
        for j in range(k + 1, stored):
            left[j] = left[j] + delta[k] * cross[k][j]
    of_steps = jnp.concatenate([-delta[k] for k in range(stored)], axis=0)
    of_slopes = jnp.concatenate([gamma * alpha[k] for k in range(stored)], axis=0)
    for r in range(4):
        at = slice(r * HALF, (r + 1) * HALF)
        mix = jnp.sum(of_steps * steps[:, at] + of_slopes * slopes[:, at], axis=0, keepdims=True)
        out[r : r + 1, :] = mix - gamma * gradient[r : r + 1, :]


def per_device(sources, targets, potential, block_map, counts, step_history, slope_history):
    src_size, tgt_size = lax.axis_size(SRC), lax.axis_size(TGT)
    blocks = potential.shape[0] // BLOCK
    own_blocks = targets.shape[0] // BLOCK
    listed = block_map.shape[1]
    stored = step_history.shape[0]
    pieces = sources.shape[0] // BLOCK
    assert pieces == 2

    packed = jnp.concatenate([sources[:BLOCK], sources[BLOCK:]], axis=1)
    mine = share(packed, TGT[0])
    core = lax.axis_index(TGT[1])
    t = targets.T
    rank = jnp.stack([lax.axis_index(TGT), core]).astype(jnp.int32)
    columns = call(
        columns_kernel,
        sds((BLOCK, HALF), jnp.bfloat16),
        [SMEM, VMEM],
        VMEM,
        [pltpu.VMEM((HALF, HALF), F32)],
    )(rank, potential.reshape(-1, HALF))
    slots = blocks * listed + UNROLL
    pairs, total = call(
        functools.partial(listing_kernel, blocks, own_blocks),
        (sds((slots,), jnp.int32), sds((1,), jnp.int32)),
        [SMEM] * 3,
        [SMEM] * 2,
    )(rank, block_map, counts)

    mine, columns, pairs, total = lax.optimization_barrier((mine, columns, pairs, total))
    other = lax.ppermute(mine, TGT[1], [(0, 1), (1, 0)])
    history = jnp.concatenate([step_history, slope_history], axis=0)
    moments = call(
        functools.partial(moments_kernel, stored),
        sds((1, HALF)),
        [VMEM],
        VMEM,
        [pltpu.VMEM((2 * stored, HALF), F32)],
    )(history)

    rows = pltpu.VMEM((blocks, BLOCK, HALF), jnp.bfloat16)
    levels = call(
        functools.partial(column_kernel, blocks, own_blocks),
        sds((src_size, 4, HALF)),
        [SMEM] * 2 + [VMEM] * 4,
        VMEM,
        [rows] + [pltpu.VMEM((8 * own_blocks + 8, BLOCK), F32)] * 2,
        COST,
    )(pairs, total, mine, other, t, columns)

    arrived = swap(levels, SRC)

    level = call(
        functools.partial(combine_kernel, src_size),
        sds((src_size, 4, HALF)),
        [VMEM],
        VMEM,
    )(arrived)
    level = swap(level, SRC)
    target_potential = (-entropy * LN2) * level.reshape(-1)

    parts = call(
        functools.partial(row_kernel, blocks, own_blocks),
        sds((tgt_size, 4, HALF)),
        [SMEM] * 3 + [VMEM] * 5,
        VMEM,
        [
            rows,
            pltpu.VMEM((blocks + 1, BLOCK, HALF), F32),
            pltpu.VMEM((tgt_size, 4, HALF), F32),
        ],
        COST,
    )(rank, pairs, total, mine, other, t, columns, level)

    ratio = blocks * src_size / (own_blocks * tgt_size)
    gradient, again, dots = call(
        functools.partial(gradient_kernel, tgt_size, ratio),
        (sds((4, HALF)), sds((4, HALF)), sds((tgt_size, 1, HALF))),
        [VMEM] * 3,
        [VMEM] * 3,
    )(swap(parts, TGT), history, moments)
    dots = call(pass_on_kernel, sds((src_size, 1, HALF)), [VMEM], VMEM)(swap(dots, TGT))
    direction = call(
        functools.partial(direction_kernel, src_size, stored), sds((4, HALF)), [VMEM] * 4, VMEM
    )(swap(dots, SRC), again, step_history, slope_history)
    return (gradient.reshape(-1), direction.reshape(-1), target_potential)


def solution(mesh):
    split = Mesh(mesh.devices.reshape(4, 8, 8, 2), ("src_0", "src_1", "tgt_0", "tgt_1"))
    in_specs = (
        P(SRC_TGT, None),
        P(TGT, None),
        P(SRC),
        P(SRC, None),
        P(SRC),
        P(None, SRC_TGT),
        P(None, SRC_TGT),
    )
    out_specs = (P(SRC_TGT), P(SRC_TGT), P(TGT))
    return jax.shard_map(
        per_device, mesh=split, in_specs=in_specs, out_specs=out_specs, check_vma=False
    )
```

```python
import functools

import jax
import jax.numpy as jnp
from jax import lax
from jax.experimental import pallas as pl
from jax.experimental.pallas import tpu as pltpu
from jax.sharding import Mesh
from jax.sharding import PartitionSpec as P

BLOCK = 256
HALF = 128
TGT = ("tgt_0", "tgt_1")
SRC = ("src_0", "src_1")
SRC_TGT = ("src_0", "src_1", "tgt_0", "tgt_1")
NEG = -1e30
LOG2E = 1.4426950408889634
LN2 = 0.6931471805599453
entropy = 0.5
SCALE = LOG2E / entropy
UNROLL = 8
PLACE = 1 << 16
WIDE = 64
F32 = jnp.float32

VMEM = pl.BlockSpec(memory_space=pltpu.VMEM)
SMEM = pl.BlockSpec(memory_space=pltpu.SMEM)


COST = pl.CostEstimate(flops=10**10, bytes_accessed=10**6, transcendentals=0)


def call(body, out_shape, ins, outs, scratch=(), cost=None):
    return pl.pallas_call(
        body,
        out_shape=out_shape,
        in_specs=ins,
        out_specs=outs,
        scratch_shapes=list(scratch),
        cost_estimate=cost,
        compiler_params=pltpu.CompilerParams(vmem_limit_bytes=24 * 2**20),
    )


def sds(shape, dtype=F32):
    return jax.ShapeDtypeStruct(shape, dtype)


def nn(a, b):
    return jnp.dot(a, b, preferred_element_type=F32)


def nt(a, b, precision=None):
    return lax.dot_general(
        a, b, (((1,), (1,)), ((), ())), precision=precision, preferred_element_type=F32
    )


def swap(x, axis):
    return lax.all_to_all(x, axis, 0, 0, tiled=True)


def share(x, axis):
    return swap(jnp.broadcast_to(x[None], (lax.axis_size(axis), *x.shape)), axis)


def pack_kernel(given, out):
    for h in range(BLOCK // HALF):
        parts = [
            jnp.transpose(given[:, b * BLOCK + h * HALF : b * BLOCK + (h + 1) * HALF])
            for b in range(2)
        ]
        tile = jnp.concatenate(parts, axis=1)
        for k in range(out.shape[0]):
            out[k, h * HALF : (h + 1) * HALF, :] = tile


def listing_kernel(blocks, own_blocks, rank, block_map, counts, pairs, total):
    first = rank[0] * own_blocks
    core = rank[1]

    def of_block(b, n):
        count = counts[b]
        far = (lax.rem(lax.shift_right_logical(b, 1), 2) != core).astype(jnp.int32)
        place = far * (blocks // 2) + 2 * lax.shift_right_logical(b, 2) + lax.rem(b, 2)
        for k in range(block_map.shape[1]):
            local = block_map[b, k] - first
            pairs[n] = place * PLACE + local
            mine = (k < count) & (local >= 0) & (local < own_blocks)
            n = n + mine.astype(jnp.int32)
        return n

    n = lax.fori_loop(0, blocks, of_block, jnp.int32(0))
    total[0] = n
    for extra in range(UNROLL):
        pairs[n + extra] = blocks * PLACE + own_blocks


def split_three(value):
    high = value.astype(jnp.bfloat16).astype(F32)
    rest = value - high
    middle = rest.astype(jnp.bfloat16).astype(F32)
    return high, middle, rest - middle


def columns_kernel(rank, pot, out, tile):
    core = rank[1]
    tile[...] = jnp.zeros(tile.shape, F32)
    ys = pot.shape[0] // 8
    for h in range(2):
        for far in range(2):
            for y in range(ys):
                for half in range(2):
                    side = 1 - core if far else core
                    parts = split_three(pot[pl.ds(8 * y + 4 * side + 2 * half + h, 1), :])
                    for k in range(3):
                        at = 4 * (2 * ys * far + 2 * y + half) + k
                        tile[at : at + 1, :] = parts[k]
        out[h * HALF : (h + 1) * HALF, :] = jnp.transpose(tile[...]).astype(jnp.bfloat16)


def turned(value, by):
    return jnp.concatenate([value[:, by:], value[:, :by]], axis=1) if by % HALF else value


def lay_out(mine, other, columns, x):
    lane = lax.broadcasted_iota(jnp.int32, (BLOCK, HALF), 1)
    ones = jnp.where((lane >= WIDE + 3) & (lane < WIDE + 6), 1.0, 0.0).astype(jnp.bfloat16)
    own = columns[...]
    place = 0
    for arrived in (mine, other):
        for y in range(arrived.shape[0]):
            piece = arrived[y]
            for half in range(2):
                parts = turned(own, (4 * place - WIDE) % HALF)
                rest = jnp.where((lane >= WIDE) & (lane < WIDE + 3), parts, ones)
                x[place] = jnp.where(lane < WIDE, turned(piece, WIDE * half), rest)
                place += 1


def target_columns(t, tb, h, extra):
    cols = t[:, pl.ds(pl.multiple_of(tb * BLOCK + h * HALF, HALF), HALF)]
    zeros = jnp.zeros((HALF - WIDE - 16, HALF), jnp.bfloat16)
    return jnp.concatenate([cols, extra.astype(jnp.bfloat16), zeros], axis=0)


def column_kernel(
    blocks, own_blocks, listed, total, mine, other, t, columns, out, x, peak, acc
):
    lay_out(mine, other, columns, x)
    peak[...] = jnp.full(peak.shape, NEG, F32)
    acc[...] = jnp.zeros(acc.shape, F32)
    live = total[0]
    row = lax.broadcasted_iota(jnp.int32, (16, HALF), 0)
    extra = jnp.where(row < 3, 1.0, 0.0)

    def turn(step, carry):
        found = []
        for u in range(UNROLL):
            pair = listed[step * UNROLL + u]
            b_all = lax.shift_right_logical(pair, 16)
            t_all = lax.bitwise_and(pair, PLACE - 1)
            b = jnp.minimum(b_all, blocks - 1)
            tb = jnp.minimum(t_all, own_blocks - 1)
            rows = x[b]
            for h in range(2):
                s = nn(rows, target_columns(t, tb, h, extra)) * SCALE
                s = s.reshape(BLOCK // 8, 8, HALF)
                top = jnp.max(s, axis=0)
                part = jnp.sum(jnp.exp2(s - top[None]), axis=0)
                found.append((t_all, h, top, part))
        for t_all, h, top, part in found:
            at = (pl.ds(pl.multiple_of(t_all * 8, 8), 8), slice(h * HALF, (h + 1) * HALF))
            old = peak[at]
            new = jnp.maximum(old, top)
            acc[at] = acc[at] * jnp.exp2(old - new) + part * jnp.exp2(top - new)
            peak[at] = new
        return carry

    lax.fori_loop(0, (live + UNROLL - 1) // UNROLL, turn, 0)

    def finish(p, carry):
        for r in range(4):
            at = (
                pl.ds(pl.multiple_of((2 * p + r // 2) * 8, 8), 8),
                slice((r % 2) * HALF, (r % 2 + 1) * HALF),
            )
            tops = peak[at]
            top = jnp.max(tops, axis=0, keepdims=True)
            whole = jnp.sum(acc[at] * jnp.exp2(tops - top), axis=0, keepdims=True)
            level = jnp.where(whole > 0.0, top + jnp.log2(jnp.maximum(whole, 1e-38)), NEG)
            out[p, r : r + 1, :] = level
        return carry

    lax.fori_loop(0, own_blocks // 2, finish, 0, unroll=4)


def combine_kernel(peers, arrived, out):
    top = arrived[0]
    for p in range(1, peers):
        top = jnp.maximum(top, arrived[p])
    whole = jnp.zeros_like(top)
    for p in range(peers):
        whole = whole + jnp.exp2(arrived[p] - top)
    level = top + jnp.log2(whole)
    for p in range(peers):
        out[p] = level


def moments_kernel(stored, history, out, square):
    total = nt(history[...], history[...], lax.Precision.HIGHEST)
    square[...] = jnp.zeros(square.shape, F32)
    square[:, : 2 * stored] = total
    lane = lax.broadcasted_iota(jnp.int32, (1, HALF), 1)
    line = jnp.zeros((1, HALF), F32)
    for k in range(stored):
        for row, place in ((k, cross_lane(k, k)), (stored + k, slope_lane(k, k))):
            kept = (lane >= stored + k) & (lane < 2 * stored)
            part = jnp.where(kept, square[row : row + 1, :], 0.0)
            line = line + pltpu.roll(part, (place - stored - k) % HALF, 1)
    out[...] = line


def row_kernel(
    blocks,
    own_blocks,
    rank,
    listed,
    total,
    mine,
    other,
    t,
    columns,
    level,
    out,
    x,
    acc,
    sums,
):
    lay_out(mine, other, columns, x)
    acc[...] = jnp.zeros(acc.shape, F32)
    live = total[0]
    row = lax.broadcasted_iota(jnp.int32, (16, HALF), 0)
    ones = jnp.where(row < 3, 1.0, 0.0)

    def turn(step, carry):
        found = []
        for u in range(UNROLL):
            pair = listed[step * UNROLL + u]
            b_all = lax.shift_right_logical(pair, 16)
            t_all = lax.bitwise_and(pair, PLACE - 1)
            b = jnp.minimum(b_all, blocks - 1)
            tb = jnp.minimum(t_all, own_blocks - 1)
            rows = x[b]
            parts = None
            for h in range(2):
                line = level[
                    lax.shift_right_logical(tb, 1), pl.ds(lax.rem(tb, 2) * 2 + h, 1), :
                ]
                extra = ones
                for k, part in enumerate(split_three((-entropy * LN2) * line)):
                    extra = jnp.where(row == 3 + k, part, extra)
                e = jnp.exp2(nn(rows, target_columns(t, tb, h, extra)) * SCALE)
                parts = e if parts is None else parts + e
            found.append((b_all, parts))
        for b_all, parts in found:
            acc[b_all] = acc[b_all] + parts
        return carry

    lax.fori_loop(0, (live + UNROLL - 1) // UNROLL, turn, 0)

    def fold(b, carry):
        for h in range(2):
            turned = jnp.transpose(acc[b, h * HALF : (h + 1) * HALF, :])
            at = pl.ds(lax.rem(b, 2) * 2 + h, 1)
            sums[lax.shift_right_logical(b, 1), at, :] = jnp.sum(turned, axis=0, keepdims=True)
        return carry

    lax.fori_loop(0, blocks, fold, 0, unroll=4)

    core = rank[1]
    place = 0
    for side in (core, 1 - core):
        for y in range(mine.shape[0]):
            out[2 * y + side] = sums[place]
            place += 1


def gradient_kernel(peers, ratio, arrived, history, moments, gradient, again, dots):
    whole = arrived[0]
    for p in range(1, peers):
        whole = whole + arrived[p]
    grad = 1.0 - ratio * whole
    gradient[...] = grad
    again[...] = grad
    rows_kept = history.shape[0]
    lane = lax.broadcasted_iota(jnp.int32, (rows_kept, HALF), 1)
    row = lax.broadcasted_iota(jnp.int32, (rows_kept, HALF), 0)
    total = jnp.zeros((rows_kept, HALF), F32)
    for q in range(4):
        total = total + history[:, q * HALF : (q + 1) * HALF] * grad[q : q + 1]
    spread = jnp.where(lane == row, jnp.sum(total, axis=1, keepdims=True), 0.0)
    value = jnp.sum(spread, axis=0, keepdims=True) + moments[...]
    for p in range(peers):
        dots[p] = value


def pass_on_kernel(arrived, out):
    value = arrived[0]
    for p in range(1, arrived.shape[0]):
        value = value + arrived[p]
    for p in range(out.shape[0]):
        out[p] = value


def cross_lane(k, m):
    return 16 + 8 * k - k * (k - 1) // 2 + m - k


def slope_lane(k, m):
    k, m = min(k, m), max(k, m)
    return 52 + 8 * k - k * (k - 1) // 2 + m - k


def direction_kernel(peers, stored, arrived, gradient, steps, slopes, out):
    sums = arrived[0]
    for p in range(1, peers):
        sums = sums + arrived[p]

    def lane(c):
        return jnp.broadcast_to(sums[:, c : c + 1], (1, HALF))

    cross = [[lane(cross_lane(k, m)) if m >= k else None for m in range(stored)] for k in range(stored)]
    slope = [[lane(slope_lane(k, m)) for m in range(stored)] for k in range(stored)]
    rho = [1.0 / cross[k][k] for k in range(stored)]
    gamma = cross[stored - 1][stored - 1] / slope[stored - 1][stored - 1]
    left = [lane(k) for k in range(stored)]
    alpha = [None] * stored
    for k in reversed(range(stored)):
        alpha[k] = left[k] * rho[k]
        for j in range(k):
            left[j] = left[j] - alpha[k] * cross[j][k]
    left = [lane(stored + k) for k in range(stored)]
    for k in reversed(range(stored)):
        left = [left[j] - alpha[k] * slope[j][k] for j in range(stored)]
    left = [gamma * value for value in left]
    delta = [None] * stored
    for k in range(stored):
        delta[k] = alpha[k] - left[k] * rho[k]
        for j in range(k + 1, stored):
            left[j] = left[j] + delta[k] * cross[k][j]
    of_steps = jnp.concatenate([-delta[k] for k in range(stored)], axis=0)
    of_slopes = jnp.concatenate([gamma * alpha[k] for k in range(stored)], axis=0)
    for r in range(4):
        at = slice(r * HALF, (r + 1) * HALF)
        mix = jnp.sum(of_steps * steps[:, at] + of_slopes * slopes[:, at], axis=0, keepdims=True)
        out[r : r + 1, :] = mix - gamma * gradient[r : r + 1, :]


def per_device(sources, targets, potential, block_map, counts, step_history, slope_history):
    src_size, tgt_size = lax.axis_size(SRC), lax.axis_size(TGT)
    blocks = potential.shape[0] // BLOCK
    own_blocks = targets.shape[0] // BLOCK
    listed = block_map.shape[1]
    stored = step_history.shape[0]
    pieces = sources.shape[0] // BLOCK
    assert pieces == 2

    packed = call(
        pack_kernel,
        sds((lax.axis_size(TGT[0]), BLOCK, HALF), jnp.bfloat16),
        [VMEM],
        VMEM,
        (),
        COST,
    )(sources.T)
    mine = swap(packed, TGT[0])
    core = lax.axis_index(TGT[1])
    t = targets.T
    rank = jnp.stack([lax.axis_index(TGT), core]).astype(jnp.int32)
    columns = call(
        columns_kernel,
        sds((BLOCK, HALF), jnp.bfloat16),
        [SMEM, VMEM],
        VMEM,
        [pltpu.VMEM((HALF, HALF), F32)],
    )(rank, potential.reshape(-1, HALF))
    slots = blocks * listed + UNROLL
    pairs, total = call(
        functools.partial(listing_kernel, blocks, own_blocks),
        (sds((slots,), jnp.int32), sds((1,), jnp.int32)),
        [SMEM] * 3,
        [SMEM] * 2,
    )(rank, block_map, counts)

    history = jnp.concatenate([step_history, slope_history], axis=0)
    moments = call(
        functools.partial(moments_kernel, stored),
        sds((1, HALF)),
        [VMEM],
        VMEM,
        [pltpu.VMEM((2 * stored, HALF), F32)],
    )(history)
    mine, columns, pairs, total, moments = lax.optimization_barrier(
        (mine, columns, pairs, total, moments)
    )
    other = lax.ppermute(mine, TGT[1], [(0, 1), (1, 0)])
    rows = pltpu.VMEM((blocks, BLOCK, HALF), jnp.bfloat16)
    levels = call(
        functools.partial(column_kernel, blocks, own_blocks),
        sds((src_size, 4, HALF)),
        [SMEM] * 2 + [VMEM] * 4,
        VMEM,
        [rows] + [pltpu.VMEM((8 * own_blocks + 8, BLOCK), F32)] * 2,
        COST,
    )(pairs, total, mine, other, t, columns)

    arrived = swap(levels, SRC)

    level = call(
        functools.partial(combine_kernel, src_size),
        sds((src_size, 4, HALF)),
        [VMEM],
        VMEM,
    )(arrived)
    level = swap(level, SRC)
    target_potential = (-entropy * LN2) * level.reshape(-1)

    parts = call(
        functools.partial(row_kernel, blocks, own_blocks),
        sds((tgt_size, 4, HALF)),
        [SMEM] * 3 + [VMEM] * 5,
        VMEM,
        [
            rows,
            pltpu.VMEM((blocks + 1, BLOCK, HALF), F32),
            pltpu.VMEM((tgt_size, 4, HALF), F32),
        ],
        COST,
    )(rank, pairs, total, mine, other, t, columns, level)

    arrived, target_potential = lax.optimization_barrier((swap(parts, TGT), target_potential))
    ratio = blocks * src_size / (own_blocks * tgt_size)
    gradient, again, dots = call(
        functools.partial(gradient_kernel, tgt_size, ratio),
        (sds((4, HALF)), sds((4, HALF)), sds((tgt_size, 1, HALF))),
        [VMEM] * 3,
        [VMEM] * 3,
    )(arrived, history, moments)
    dots = call(pass_on_kernel, sds((src_size, 1, HALF)), [VMEM], VMEM)(swap(dots, TGT))
    direction = call(
        functools.partial(direction_kernel, src_size, stored), sds((4, HALF)), [VMEM] * 4, VMEM
    )(swap(dots, SRC), again, step_history, slope_history)
    return (gradient.reshape(-1), direction.reshape(-1), target_potential)


def solution(mesh):
    split = Mesh(mesh.devices.reshape(4, 8, 8, 2), ("src_0", "src_1", "tgt_0", "tgt_1"))
    in_specs = (
        P(SRC_TGT, None),
        P(TGT, None),
        P(SRC),
        P(SRC, None),
        P(SRC),
        P(None, SRC_TGT),
        P(None, SRC_TGT),
    )
    out_specs = (P(SRC_TGT), P(SRC_TGT), P(TGT))
    return jax.shard_map(
        per_device, mesh=split, in_specs=in_specs, out_specs=out_specs, check_vma=False
    )
```

```python
import functools

import jax
import jax.numpy as jnp
from jax import lax
from jax.experimental import pallas as pl
from jax.experimental.pallas import tpu as pltpu
from jax.sharding import Mesh
from jax.sharding import PartitionSpec as P

BLOCK = 256
HALF = 128
TGT = ("tgt_0", "tgt_1")
SRC = ("src_0", "src_1")
SRC_TGT = ("src_0", "src_1", "tgt_0", "tgt_1")
NEG = -1e30
LOG2E = 1.4426950408889634
LN2 = 0.6931471805599453
entropy = 0.5
SCALE = LOG2E / entropy
UNROLL = 12
PLACE = 1 << 16
WIDE = 64
F32 = jnp.float32

VMEM = pl.BlockSpec(memory_space=pltpu.VMEM)
SMEM = pl.BlockSpec(memory_space=pltpu.SMEM)


COST = pl.CostEstimate(flops=10**10, bytes_accessed=10**6, transcendentals=0)


def call(body, out_shape, ins, outs, scratch=(), cost=None):
    return pl.pallas_call(
        body,
        out_shape=out_shape,
        in_specs=ins,
        out_specs=outs,
        scratch_shapes=list(scratch),
        cost_estimate=cost,
        compiler_params=pltpu.CompilerParams(vmem_limit_bytes=24 * 2**20),
    )


def sds(shape, dtype=F32):
    return jax.ShapeDtypeStruct(shape, dtype)


def nn(a, b):
    return jnp.dot(a, b, preferred_element_type=F32)


def nt(a, b, precision=None):
    return lax.dot_general(
        a, b, (((1,), (1,)), ((), ())), precision=precision, preferred_element_type=F32
    )


def swap(x, axis):
    return lax.all_to_all(x, axis, 0, 0, tiled=True)


def share(x, axis):
    return swap(jnp.broadcast_to(x[None], (lax.axis_size(axis), *x.shape)), axis)


def pack_kernel(given, out):
    for h in range(BLOCK // HALF):
        parts = [
            jnp.transpose(given[:, b * BLOCK + h * HALF : b * BLOCK + (h + 1) * HALF])
            for b in range(2)
        ]
        tile = jnp.concatenate(parts, axis=1)
        for k in range(out.shape[0]):
            out[k, h * HALF : (h + 1) * HALF, :] = tile


def listing_kernel(blocks, own_blocks, rank, block_map, counts, pairs, total):
    first = rank[0] * own_blocks
    core = rank[1]

    def of_block(b, n):
        count = counts[b]
        far = (lax.rem(lax.shift_right_logical(b, 1), 2) != core).astype(jnp.int32)
        place = far * (blocks // 2) + 2 * lax.shift_right_logical(b, 2) + lax.rem(b, 2)
        for k in range(block_map.shape[1]):
            local = block_map[b, k] - first
            pairs[n] = place * PLACE + local
            mine = (k < count) & (local >= 0) & (local < own_blocks)
            n = n + mine.astype(jnp.int32)
        return n

    n = lax.fori_loop(0, blocks, of_block, jnp.int32(0))
    total[0] = n
    for extra in range(UNROLL):
        pairs[n + extra] = blocks * PLACE + own_blocks


def split_three(value):
    high = value.astype(jnp.bfloat16).astype(F32)
    rest = value - high
    middle = rest.astype(jnp.bfloat16).astype(F32)
    return high, middle, rest - middle


def columns_kernel(rank, pot, out, tile):
    core = rank[1]
    tile[...] = jnp.zeros(tile.shape, F32)
    ys = pot.shape[0] // 8
    for h in range(2):
        for far in range(2):
            for y in range(ys):
                for half in range(2):
                    side = 1 - core if far else core
                    parts = split_three(pot[pl.ds(8 * y + 4 * side + 2 * half + h, 1), :])
                    for k in range(3):
                        at = 4 * (2 * ys * far + 2 * y + half) + k
                        tile[at : at + 1, :] = parts[k]
        out[h * HALF : (h + 1) * HALF, :] = jnp.transpose(tile[...]).astype(jnp.bfloat16)


def turned(value, by):
    return jnp.concatenate([value[:, by:], value[:, :by]], axis=1) if by % HALF else value


def lay_out(mine, other, columns, x):
    lane = lax.broadcasted_iota(jnp.int32, (BLOCK, HALF), 1)
    ones = jnp.where((lane >= WIDE + 3) & (lane < WIDE + 6), 1.0, 0.0).astype(jnp.bfloat16)
    own = columns[...]
    place = 0
    for arrived in (mine, other):
        for y in range(arrived.shape[0]):
            piece = arrived[y]
            for half in range(2):
                parts = turned(own, (4 * place - WIDE) % HALF)
                rest = jnp.where((lane >= WIDE) & (lane < WIDE + 3), parts, ones)
                x[place] = jnp.where(lane < WIDE, turned(piece, WIDE * half), rest)
                place += 1


def target_columns(t, tb, h, extra):
    cols = t[:, pl.ds(pl.multiple_of(tb * BLOCK + h * HALF, HALF), HALF)]
    zeros = jnp.zeros((HALF - WIDE - 16, HALF), jnp.bfloat16)
    return jnp.concatenate([cols, extra.astype(jnp.bfloat16), zeros], axis=0)


def column_kernel(
    blocks, own_blocks, listed, total, mine, other, t, columns, out, x, peak, acc
):
    lay_out(mine, other, columns, x)
    peak[...] = jnp.full(peak.shape, NEG, F32)
    acc[...] = jnp.zeros(acc.shape, F32)
    live = total[0]
    row = lax.broadcasted_iota(jnp.int32, (16, HALF), 0)
    extra = jnp.where(row < 3, 1.0, 0.0)

    def turn(step, carry):
        found = []
        for u in range(UNROLL):
            pair = listed[step * UNROLL + u]
            b_all = lax.shift_right_logical(pair, 16)
            t_all = lax.bitwise_and(pair, PLACE - 1)
            b = jnp.minimum(b_all, blocks - 1)
            tb = jnp.minimum(t_all, own_blocks - 1)
            rows = x[b]
            for h in range(2):
                s = nn(rows, target_columns(t, tb, h, extra)) * SCALE
                s = s.reshape(BLOCK // 8, 8, HALF)
                top = jnp.max(s, axis=0)
                part = jnp.sum(jnp.exp2(s - top[None]), axis=0)
                found.append((t_all, h, top, part))
        for t_all, h, top, part in found:
            at = (pl.ds(pl.multiple_of(t_all * 8, 8), 8), slice(h * HALF, (h + 1) * HALF))
            old = peak[at]
            new = jnp.maximum(old, top)
            acc[at] = acc[at] * jnp.exp2(old - new) + part * jnp.exp2(top - new)
            peak[at] = new
        return carry

    lax.fori_loop(0, (live + UNROLL - 1) // UNROLL, turn, 0)

    def finish(p, carry):
        for r in range(4):
            at = (
                pl.ds(pl.multiple_of((2 * p + r // 2) * 8, 8), 8),
                slice((r % 2) * HALF, (r % 2 + 1) * HALF),
            )
            tops = peak[at]
            top = jnp.max(tops, axis=0, keepdims=True)
            whole = jnp.sum(acc[at] * jnp.exp2(tops - top), axis=0, keepdims=True)
            level = jnp.where(whole > 0.0, top + jnp.log2(jnp.maximum(whole, 1e-38)), NEG)
            out[p, r : r + 1, :] = level
        return carry

    lax.fori_loop(0, own_blocks // 2, finish, 0, unroll=4)


def combine_kernel(peers, arrived, out):
    top = arrived[0]
    for p in range(1, peers):
        top = jnp.maximum(top, arrived[p])
    whole = jnp.zeros_like(top)
    for p in range(peers):
        whole = whole + jnp.exp2(arrived[p] - top)
    level = top + jnp.log2(whole)
    for p in range(peers):
        out[p] = level


def moments_kernel(stored, history, out, square):
    total = nt(history[...], history[...], lax.Precision.HIGHEST)
    square[...] = jnp.zeros(square.shape, F32)
    square[:, : 2 * stored] = total
    lane = lax.broadcasted_iota(jnp.int32, (1, HALF), 1)
    line = jnp.zeros((1, HALF), F32)
    for k in range(stored):
        for row, place in ((k, cross_lane(k, k)), (stored + k, slope_lane(k, k))):
            kept = (lane >= stored + k) & (lane < 2 * stored)
            part = jnp.where(kept, square[row : row + 1, :], 0.0)
            line = line + pltpu.roll(part, (place - stored - k) % HALF, 1)
    out[...] = line


def row_kernel(
    blocks,
    own_blocks,
    rank,
    listed,
    total,
    mine,
    other,
    t,
    columns,
    level,
    out,
    x,
    acc,
    sums,
):
    lay_out(mine, other, columns, x)
    acc[...] = jnp.zeros(acc.shape, F32)
    live = total[0]
    row = lax.broadcasted_iota(jnp.int32, (16, HALF), 0)
    ones = jnp.where(row < 3, 1.0, 0.0)

    def turn(step, carry):
        found = []
        for u in range(UNROLL):
            pair = listed[step * UNROLL + u]
            b_all = lax.shift_right_logical(pair, 16)
            t_all = lax.bitwise_and(pair, PLACE - 1)
            b = jnp.minimum(b_all, blocks - 1)
            tb = jnp.minimum(t_all, own_blocks - 1)
            rows = x[b]
            parts = None
            for h in range(2):
                line = level[
                    lax.shift_right_logical(tb, 1), pl.ds(lax.rem(tb, 2) * 2 + h, 1), :
                ]
                extra = ones
                for k, part in enumerate(split_three((-entropy * LN2) * line)):
                    extra = jnp.where(row == 3 + k, part, extra)
                e = jnp.exp2(nn(rows, target_columns(t, tb, h, extra)) * SCALE)
                parts = e if parts is None else parts + e
            found.append((b_all, parts))
        for b_all, parts in found:
            acc[b_all] = acc[b_all] + parts
        return carry

    lax.fori_loop(0, (live + UNROLL - 1) // UNROLL, turn, 0)

    def fold(b, carry):
        for h in range(2):
            turned = jnp.transpose(acc[b, h * HALF : (h + 1) * HALF, :])
            at = pl.ds(lax.rem(b, 2) * 2 + h, 1)
            sums[lax.shift_right_logical(b, 1), at, :] = jnp.sum(turned, axis=0, keepdims=True)
        return carry

    lax.fori_loop(0, blocks, fold, 0, unroll=4)

    core = rank[1]
    place = 0
    for side in (core, 1 - core):
        for y in range(mine.shape[0]):
            out[2 * y + side] = sums[place]
            place += 1


def gradient_kernel(peers, ratio, arrived, history, moments, gradient, again, dots):
    whole = arrived[0]
    for p in range(1, peers):
        whole = whole + arrived[p]
    grad = 1.0 - ratio * whole
    gradient[...] = grad
    again[...] = grad
    rows_kept = history.shape[0]
    lane = lax.broadcasted_iota(jnp.int32, (rows_kept, HALF), 1)
    row = lax.broadcasted_iota(jnp.int32, (rows_kept, HALF), 0)
    total = jnp.zeros((rows_kept, HALF), F32)
    for q in range(4):
        total = total + history[:, q * HALF : (q + 1) * HALF] * grad[q : q + 1]
    spread = jnp.where(lane == row, jnp.sum(total, axis=1, keepdims=True), 0.0)
    value = jnp.sum(spread, axis=0, keepdims=True) + moments[...]
    for p in range(peers):
        dots[p] = value


def pass_on_kernel(arrived, out):
    value = arrived[0]
    for p in range(1, arrived.shape[0]):
        value = value + arrived[p]
    for p in range(out.shape[0]):
        out[p] = value


def cross_lane(k, m):
    return 16 + 8 * k - k * (k - 1) // 2 + m - k


def slope_lane(k, m):
    k, m = min(k, m), max(k, m)
    return 52 + 8 * k - k * (k - 1) // 2 + m - k


def direction_kernel(peers, stored, arrived, gradient, steps, slopes, out):
    sums = arrived[0]
    for p in range(1, peers):
        sums = sums + arrived[p]

    def lane(c):
        return jnp.broadcast_to(sums[:, c : c + 1], (1, HALF))

    cross = [[lane(cross_lane(k, m)) if m >= k else None for m in range(stored)] for k in range(stored)]
    slope = [[lane(slope_lane(k, m)) for m in range(stored)] for k in range(stored)]
    rho = [1.0 / cross[k][k] for k in range(stored)]
    gamma = cross[stored - 1][stored - 1] / slope[stored - 1][stored - 1]
    left = [lane(k) for k in range(stored)]
    alpha = [None] * stored
    for k in reversed(range(stored)):
        alpha[k] = left[k] * rho[k]
        for j in range(k):
            left[j] = left[j] - alpha[k] * cross[j][k]
    left = [lane(stored + k) for k in range(stored)]
    for k in reversed(range(stored)):
        left = [left[j] - alpha[k] * slope[j][k] for j in range(stored)]
    left = [gamma * value for value in left]
    delta = [None] * stored
    for k in range(stored):
        delta[k] = alpha[k] - left[k] * rho[k]
        for j in range(k + 1, stored):
            left[j] = left[j] + delta[k] * cross[k][j]
    of_steps = jnp.concatenate([-delta[k] for k in range(stored)], axis=0)
    of_slopes = jnp.concatenate([gamma * alpha[k] for k in range(stored)], axis=0)
    for r in range(4):
        at = slice(r * HALF, (r + 1) * HALF)
        mix = jnp.sum(of_steps * steps[:, at] + of_slopes * slopes[:, at], axis=0, keepdims=True)
        out[r : r + 1, :] = mix - gamma * gradient[r : r + 1, :]


def per_device(sources, targets, potential, block_map, counts, step_history, slope_history):
    src_size, tgt_size = lax.axis_size(SRC), lax.axis_size(TGT)
    blocks = potential.shape[0] // BLOCK
    own_blocks = targets.shape[0] // BLOCK
    listed = block_map.shape[1]
    stored = step_history.shape[0]
    pieces = sources.shape[0] // BLOCK
    assert pieces == 2

    packed = call(
        pack_kernel,
        sds((lax.axis_size(TGT[0]), BLOCK, HALF), jnp.bfloat16),
        [VMEM],
        VMEM,
        (),
        COST,
    )(sources.T)
    mine = swap(packed, TGT[0])
    core = lax.axis_index(TGT[1])
    t = targets.T
    rank = jnp.stack([lax.axis_index(TGT), core]).astype(jnp.int32)
    columns = call(
        columns_kernel,
        sds((BLOCK, HALF), jnp.bfloat16),
        [SMEM, VMEM],
        VMEM,
        [pltpu.VMEM((HALF, HALF), F32)],
    )(rank, potential.reshape(-1, HALF))
    slots = blocks * listed + UNROLL
    pairs, total = call(
        functools.partial(listing_kernel, blocks, own_blocks),
        (sds((slots,), jnp.int32), sds((1,), jnp.int32)),
        [SMEM] * 3,
        [SMEM] * 2,
    )(rank, block_map, counts)

    history = jnp.concatenate([step_history, slope_history], axis=0)
    moments = call(
        functools.partial(moments_kernel, stored),
        sds((1, HALF)),
        [VMEM],
        VMEM,
        [pltpu.VMEM((2 * stored, HALF), F32)],
    )(history)
    mine, columns, pairs, total, moments = lax.optimization_barrier(
        (mine, columns, pairs, total, moments)
    )
    other = lax.ppermute(mine, TGT[1], [(0, 1), (1, 0)])
    rows = pltpu.VMEM((blocks, BLOCK, HALF), jnp.bfloat16)
    levels = call(
        functools.partial(column_kernel, blocks, own_blocks),
        sds((src_size, 4, HALF)),
        [SMEM] * 2 + [VMEM] * 4,
        VMEM,
        [rows] + [pltpu.VMEM((8 * own_blocks + 8, BLOCK), F32)] * 2,
        COST,
    )(pairs, total, mine, other, t, columns)

    arrived = swap(levels, SRC)

    level = call(
        functools.partial(combine_kernel, src_size),
        sds((src_size, 4, HALF)),
        [VMEM],
        VMEM,
    )(arrived)
    level = swap(level, SRC)
    target_potential = (-entropy * LN2) * level.reshape(-1)

    parts = call(
        functools.partial(row_kernel, blocks, own_blocks),
        sds((tgt_size, 4, HALF)),
        [SMEM] * 3 + [VMEM] * 5,
        VMEM,
        [
            rows,
            pltpu.VMEM((blocks + 1, BLOCK, HALF), F32),
            pltpu.VMEM((tgt_size, 4, HALF), F32),
        ],
        COST,
    )(rank, pairs, total, mine, other, t, columns, level)

    arrived, target_potential = lax.optimization_barrier((swap(parts, TGT), target_potential))
    ratio = blocks * src_size / (own_blocks * tgt_size)
    gradient, again, dots = call(
        functools.partial(gradient_kernel, tgt_size, ratio),
        (sds((4, HALF)), sds((4, HALF)), sds((tgt_size, 1, HALF))),
        [VMEM] * 3,
        [VMEM] * 3,
    )(arrived, history, moments)
    dots = call(pass_on_kernel, sds((src_size, 1, HALF)), [VMEM], VMEM)(swap(dots, TGT))
    direction = call(
        functools.partial(direction_kernel, src_size, stored), sds((4, HALF)), [VMEM] * 4, VMEM
    )(swap(dots, SRC), again, step_history, slope_history)
    return (gradient.reshape(-1), direction.reshape(-1), target_potential)


def solution(mesh):
    split = Mesh(mesh.devices.reshape(4, 8, 8, 2), ("src_0", "src_1", "tgt_0", "tgt_1"))
    in_specs = (
        P(SRC_TGT, None),
        P(TGT, None),
        P(SRC),
        P(SRC, None),
        P(SRC),
        P(None, SRC_TGT),
        P(None, SRC_TGT),
    )
    out_specs = (P(SRC_TGT), P(SRC_TGT), P(TGT))
    return jax.shard_map(
        per_device, mesh=split, in_specs=in_specs, out_specs=out_specs, check_vma=False
    )
```

```python
import functools

import jax
import jax.numpy as jnp
from jax import lax
from jax.experimental import pallas as pl
from jax.experimental.pallas import tpu as pltpu
from jax.sharding import Mesh
from jax.sharding import PartitionSpec as P

BLOCK = 256
HALF = 128
TGT = ("tgt_0", "tgt_1")
SRC = ("src_0", "src_1")
SRC_TGT = ("src_0", "src_1", "tgt_0", "tgt_1")
NEG = -1e30
LOG2E = 1.4426950408889634
LN2 = 0.6931471805599453
entropy = 0.5
SCALE = LOG2E / entropy
UNROLL = 12
PLACE = 1 << 16
WIDE = 64
F32 = jnp.float32

VMEM = pl.BlockSpec(memory_space=pltpu.VMEM)
SMEM = pl.BlockSpec(memory_space=pltpu.SMEM)


COST = pl.CostEstimate(flops=10**10, bytes_accessed=10**6, transcendentals=0)


def call(body, out_shape, ins, outs, scratch=(), cost=None):
    return pl.pallas_call(
        body,
        out_shape=out_shape,
        in_specs=ins,
        out_specs=outs,
        scratch_shapes=list(scratch),
        cost_estimate=cost,
        compiler_params=pltpu.CompilerParams(vmem_limit_bytes=24 * 2**20),
    )


def sds(shape, dtype=F32):
    return jax.ShapeDtypeStruct(shape, dtype)


def nn(a, b):
    return jnp.dot(a, b, preferred_element_type=F32)


def nt(a, b, precision=None):
    return lax.dot_general(
        a, b, (((1,), (1,)), ((), ())), precision=precision, preferred_element_type=F32
    )


def swap(x, axis):
    return lax.all_to_all(x, axis, 0, 0, tiled=True)


def share(x, axis):
    return swap(jnp.broadcast_to(x[None], (lax.axis_size(axis), *x.shape)), axis)


def pack_kernel(given, out):
    for h in range(BLOCK // HALF):
        parts = [
            jnp.transpose(given[:, b * BLOCK + h * HALF : b * BLOCK + (h + 1) * HALF])
            for b in range(2)
        ]
        tile = jnp.concatenate(parts, axis=1)
        for k in range(out.shape[0]):
            out[k, h * HALF : (h + 1) * HALF, :] = tile


def listing_kernel(blocks, own_blocks, rank, block_map, counts, pairs, total):
    first = rank[0] * own_blocks
    core = rank[1]

    def of_block(b, n):
        count = counts[b]
        far = (lax.rem(lax.shift_right_logical(b, 1), 2) != core).astype(jnp.int32)
        place = far * (blocks // 2) + 2 * lax.shift_right_logical(b, 2) + lax.rem(b, 2)
        for k in range(block_map.shape[1]):
            local = block_map[b, k] - first
            pairs[n] = place * PLACE + local
            mine = (k < count) & (local >= 0) & (local < own_blocks)
            n = n + mine.astype(jnp.int32)
        return n

    n = lax.fori_loop(0, blocks, of_block, jnp.int32(0))
    total[0] = n
    for extra in range(UNROLL):
        pairs[n + extra] = blocks * PLACE + own_blocks


def split_three(value):
    high = value.astype(jnp.bfloat16).astype(F32)
    rest = value - high
    middle = rest.astype(jnp.bfloat16).astype(F32)
    return high, middle, rest - middle


def columns_kernel(rank, pot, out, tile):
    core = rank[1]
    tile[...] = jnp.zeros(tile.shape, F32)
    ys = pot.shape[0] // 8
    for h in range(2):
        for far in range(2):
            for y in range(ys):
                for half in range(2):
                    side = 1 - core if far else core
                    parts = split_three(pot[pl.ds(8 * y + 4 * side + 2 * half + h, 1), :])
                    for k in range(3):
                        at = 4 * (2 * ys * far + 2 * y + half) + k
                        tile[at : at + 1, :] = parts[k]
        out[h * HALF : (h + 1) * HALF, :] = jnp.transpose(tile[...]).astype(jnp.bfloat16)


def turned(value, by):
    return jnp.concatenate([value[:, by:], value[:, :by]], axis=1) if by % HALF else value


def lay_out(mine, other, columns, x):
    lane = lax.broadcasted_iota(jnp.int32, (BLOCK, HALF), 1)
    ones = jnp.where((lane >= WIDE + 3) & (lane < WIDE + 6), 1.0, 0.0).astype(jnp.bfloat16)
    own = columns[...]
    place = 0
    for arrived in (mine, other):
        for y in range(arrived.shape[0]):
            piece = arrived[y]
            for half in range(2):
                parts = turned(own, (4 * place - WIDE) % HALF)
                rest = jnp.where((lane >= WIDE) & (lane < WIDE + 3), parts, ones)
                x[place] = jnp.where(lane < WIDE, turned(piece, WIDE * half), rest)
                place += 1


def target_columns(t, tb, h, extra):
    cols = t[:, pl.ds(pl.multiple_of(tb * BLOCK + h * HALF, HALF), HALF)]
    zeros = jnp.zeros((HALF - WIDE - 16, HALF), jnp.bfloat16)
    return jnp.concatenate([cols, extra.astype(jnp.bfloat16), zeros], axis=0)


def column_kernel(
    blocks, own_blocks, listed, total, mine, other, t, columns, out, x, peak, acc
):
    lay_out(mine, other, columns, x)
    peak[...] = jnp.full(peak.shape, NEG, F32)
    acc[...] = jnp.zeros(acc.shape, F32)
    live = total[0]
    row = lax.broadcasted_iota(jnp.int32, (16, HALF), 0)
    extra = jnp.where(row < 3, 1.0, 0.0)

    def turn(step, carry):
        found = []
        for u in range(UNROLL):
            pair = listed[step * UNROLL + u]
            b_all = lax.shift_right_logical(pair, 16)
            t_all = lax.bitwise_and(pair, PLACE - 1)
            b = jnp.minimum(b_all, blocks - 1)
            tb = jnp.minimum(t_all, own_blocks - 1)
            rows = x[b]
            for h in range(2):
                s = nn(rows, target_columns(t, tb, h, extra)) * SCALE
                s = s.reshape(BLOCK // 8, 8, HALF)
                top = jnp.max(s, axis=0)
                part = jnp.sum(jnp.exp2(s - top[None]), axis=0)
                found.append((t_all, h, top, part))
        for t_all, h, top, part in found:
            at = (pl.ds(pl.multiple_of(t_all * 8, 8), 8), slice(h * HALF, (h + 1) * HALF))
            old = peak[at]
            new = jnp.maximum(old, top)
            acc[at] = acc[at] * jnp.exp2(old - new) + part * jnp.exp2(top - new)
            peak[at] = new
        return carry

    lax.fori_loop(0, (live + UNROLL - 1) // UNROLL, turn, 0)

    def finish(p, carry):
        for r in range(4):
            at = (
                pl.ds(pl.multiple_of((2 * p + r // 2) * 8, 8), 8),
                slice((r % 2) * HALF, (r % 2 + 1) * HALF),
            )
            tops = peak[at]
            top = jnp.max(tops, axis=0, keepdims=True)
            whole = jnp.sum(acc[at] * jnp.exp2(tops - top), axis=0, keepdims=True)
            level = jnp.where(whole > 0.0, top + jnp.log2(jnp.maximum(whole, 1e-38)), NEG)
            out[p, r : r + 1, :] = level
        return carry

    lax.fori_loop(0, own_blocks // 2, finish, 0, unroll=4)


def combine_kernel(peers, arrived, out):
    top = arrived[0]
    for p in range(1, peers):
        top = jnp.maximum(top, arrived[p])
    whole = jnp.zeros_like(top)
    for p in range(peers):
        whole = whole + jnp.exp2(arrived[p] - top)
    level = top + jnp.log2(whole)
    for p in range(peers):
        out[p] = level


def moments_kernel(stored, history, out, square):
    total = nt(history[...], history[...], lax.Precision.HIGHEST)
    square[...] = jnp.zeros(square.shape, F32)
    square[:, : 2 * stored] = total
    lane = lax.broadcasted_iota(jnp.int32, (1, HALF), 1)
    line = jnp.zeros((1, HALF), F32)
    for k in range(stored):
        for row, place in ((k, cross_lane(k, k)), (stored + k, slope_lane(k, k))):
            kept = (lane >= stored + k) & (lane < 2 * stored)
            part = jnp.where(kept, square[row : row + 1, :], 0.0)
            line = line + pltpu.roll(part, (place - stored - k) % HALF, 1)
    out[...] = line


def row_kernel(
    blocks,
    own_blocks,
    rank,
    listed,
    total,
    x,
    t,
    level,
    out,
    acc,
    sums,
):
    acc[...] = jnp.zeros(acc.shape, F32)
    live = total[0]
    row = lax.broadcasted_iota(jnp.int32, (16, HALF), 0)
    ones = jnp.where(row < 3, 1.0, 0.0)

    def turn(step, carry):
        found = []
        for u in range(UNROLL):
            pair = listed[step * UNROLL + u]
            b_all = lax.shift_right_logical(pair, 16)
            t_all = lax.bitwise_and(pair, PLACE - 1)
            b = jnp.minimum(b_all, blocks - 1)
            tb = jnp.minimum(t_all, own_blocks - 1)
            rows = x[b]
            parts = None
            for h in range(2):
                line = level[
                    lax.shift_right_logical(tb, 1), pl.ds(lax.rem(tb, 2) * 2 + h, 1), :
                ]
                extra = ones
                for k, part in enumerate(split_three((-entropy * LN2) * line)):
                    extra = jnp.where(row == 3 + k, part, extra)
                e = jnp.exp2(nn(rows, target_columns(t, tb, h, extra)) * SCALE)
                parts = e if parts is None else parts + e
            found.append((b_all, parts))
        for b_all, parts in found:
            acc[b_all] = acc[b_all] + parts
        return carry

    lax.fori_loop(0, (live + UNROLL - 1) // UNROLL, turn, 0)

    def fold(b, carry):
        for h in range(2):
            turned = jnp.transpose(acc[b, h * HALF : (h + 1) * HALF, :])
            at = pl.ds(lax.rem(b, 2) * 2 + h, 1)
            sums[lax.shift_right_logical(b, 1), at, :] = jnp.sum(turned, axis=0, keepdims=True)
        return carry

    lax.fori_loop(0, blocks, fold, 0, unroll=4)

    core = rank[1]
    place = 0
    for side in (core, 1 - core):
        for y in range(blocks // 4):
            out[2 * y + side] = sums[place]
            place += 1


def gradient_kernel(peers, ratio, arrived, history, moments, gradient, again, dots):
    whole = arrived[0]
    for p in range(1, peers):
        whole = whole + arrived[p]
    grad = 1.0 - ratio * whole
    gradient[...] = grad
    again[...] = grad
    rows_kept = history.shape[0]
    lane = lax.broadcasted_iota(jnp.int32, (rows_kept, HALF), 1)
    row = lax.broadcasted_iota(jnp.int32, (rows_kept, HALF), 0)
    total = jnp.zeros((rows_kept, HALF), F32)
    for q in range(4):
        total = total + history[:, q * HALF : (q + 1) * HALF] * grad[q : q + 1]
    spread = jnp.where(lane == row, jnp.sum(total, axis=1, keepdims=True), 0.0)
    value = jnp.sum(spread, axis=0, keepdims=True) + moments[...]
    for p in range(peers):
        dots[p] = value


def pass_on_kernel(arrived, out):
    value = arrived[0]
    for p in range(1, arrived.shape[0]):
        value = value + arrived[p]
    for p in range(out.shape[0]):
        out[p] = value


def cross_lane(k, m):
    return 16 + 8 * k - k * (k - 1) // 2 + m - k


def slope_lane(k, m):
    k, m = min(k, m), max(k, m)
    return 52 + 8 * k - k * (k - 1) // 2 + m - k


def direction_kernel(peers, stored, arrived, gradient, steps, slopes, out):
    sums = arrived[0]
    for p in range(1, peers):
        sums = sums + arrived[p]

    def lane(c):
        return jnp.broadcast_to(sums[:, c : c + 1], (1, HALF))

    cross = [[lane(cross_lane(k, m)) if m >= k else None for m in range(stored)] for k in range(stored)]
    slope = [[lane(slope_lane(k, m)) for m in range(stored)] for k in range(stored)]
    rho = [1.0 / cross[k][k] for k in range(stored)]
    gamma = cross[stored - 1][stored - 1] / slope[stored - 1][stored - 1]
    left = [lane(k) for k in range(stored)]
    alpha = [None] * stored
    for k in reversed(range(stored)):
        alpha[k] = left[k] * rho[k]
        for j in range(k):
            left[j] = left[j] - alpha[k] * cross[j][k]
    left = [lane(stored + k) for k in range(stored)]
    for k in reversed(range(stored)):
        left = [left[j] - alpha[k] * slope[j][k] for j in range(stored)]
    left = [gamma * value for value in left]
    delta = [None] * stored
    for k in range(stored):
        delta[k] = alpha[k] - left[k] * rho[k]
        for j in range(k + 1, stored):
            left[j] = left[j] + delta[k] * cross[k][j]
    of_steps = jnp.concatenate([-delta[k] for k in range(stored)], axis=0)
    of_slopes = jnp.concatenate([gamma * alpha[k] for k in range(stored)], axis=0)
    for r in range(4):
        at = slice(r * HALF, (r + 1) * HALF)
        mix = jnp.sum(of_steps * steps[:, at] + of_slopes * slopes[:, at], axis=0, keepdims=True)
        out[r : r + 1, :] = mix - gamma * gradient[r : r + 1, :]


def per_device(sources, targets, potential, block_map, counts, step_history, slope_history):
    src_size, tgt_size = lax.axis_size(SRC), lax.axis_size(TGT)
    blocks = potential.shape[0] // BLOCK
    own_blocks = targets.shape[0] // BLOCK
    listed = block_map.shape[1]
    stored = step_history.shape[0]
    pieces = sources.shape[0] // BLOCK
    assert pieces == 2

    packed = call(
        pack_kernel,
        sds((lax.axis_size(TGT[0]), BLOCK, HALF), jnp.bfloat16),
        [VMEM],
        VMEM,
        (),
        COST,
    )(sources.T)
    mine = swap(packed, TGT[0])
    core = lax.axis_index(TGT[1])
    t = targets.T
    rank = jnp.stack([lax.axis_index(TGT), core]).astype(jnp.int32)
    columns = call(
        columns_kernel,
        sds((BLOCK, HALF), jnp.bfloat16),
        [SMEM, VMEM],
        VMEM,
        [pltpu.VMEM((HALF, HALF), F32)],
    )(rank, potential.reshape(-1, HALF))
    slots = blocks * listed + UNROLL
    pairs, total = call(
        functools.partial(listing_kernel, blocks, own_blocks),
        (sds((slots,), jnp.int32), sds((1,), jnp.int32)),
        [SMEM] * 3,
        [SMEM] * 2,
    )(rank, block_map, counts)

    history = jnp.concatenate([step_history, slope_history], axis=0)
    moments = call(
        functools.partial(moments_kernel, stored),
        sds((1, HALF)),
        [VMEM],
        VMEM,
        [pltpu.VMEM((2 * stored, HALF), F32)],
    )(history)
    mine, columns, pairs, total, moments = lax.optimization_barrier(
        (mine, columns, pairs, total, moments)
    )
    other = lax.ppermute(mine, TGT[1], [(0, 1), (1, 0)])
    levels, x = call(
        functools.partial(column_kernel, blocks, own_blocks),
        (sds((src_size, 4, HALF)), sds((blocks, BLOCK, HALF), jnp.bfloat16)),
        [SMEM] * 2 + [VMEM] * 4,
        [VMEM] * 2,
        [pltpu.VMEM((8 * own_blocks + 8, BLOCK), F32)] * 2,
        COST,
    )(pairs, total, mine, other, t, columns)

    arrived = swap(levels, SRC)

    level = call(
        functools.partial(combine_kernel, src_size),
        sds((src_size, 4, HALF)),
        [VMEM],
        VMEM,
    )(arrived)
    level = swap(level, SRC)
    target_potential = (-entropy * LN2) * level.reshape(-1)

    parts = call(
        functools.partial(row_kernel, blocks, own_blocks),
        sds((tgt_size, 4, HALF)),
        [SMEM] * 3 + [VMEM] * 3,
        VMEM,
        [
            pltpu.VMEM((blocks + 1, BLOCK, HALF), F32),
            pltpu.VMEM((tgt_size, 4, HALF), F32),
        ],
        COST,
    )(rank, pairs, total, x, t, level)

    arrived, target_potential = lax.optimization_barrier((swap(parts, TGT), target_potential))
    ratio = blocks * src_size / (own_blocks * tgt_size)
    gradient, again, dots = call(
        functools.partial(gradient_kernel, tgt_size, ratio),
        (sds((4, HALF)), sds((4, HALF)), sds((tgt_size, 1, HALF))),
        [VMEM] * 3,
        [VMEM] * 3,
    )(arrived, history, moments)
    dots = call(pass_on_kernel, sds((src_size, 1, HALF)), [VMEM], VMEM)(swap(dots, TGT))
    direction = call(
        functools.partial(direction_kernel, src_size, stored), sds((4, HALF)), [VMEM] * 4, VMEM
    )(swap(dots, SRC), again, step_history, slope_history)
    return (gradient.reshape(-1), direction.reshape(-1), target_potential)


def solution(mesh):
    split = Mesh(mesh.devices.reshape(4, 8, 8, 2), ("src_0", "src_1", "tgt_0", "tgt_1"))
    in_specs = (
        P(SRC_TGT, None),
        P(TGT, None),
        P(SRC),
        P(SRC, None),
        P(SRC),
        P(None, SRC_TGT),
        P(None, SRC_TGT),
    )
    out_specs = (P(SRC_TGT), P(SRC_TGT), P(TGT))
    return jax.shard_map(
        per_device, mesh=split, in_specs=in_specs, out_specs=out_specs, check_vma=False
    )
```
